512 devices in a mesh: sec: 32 (over y, x), ch: 16 (over z, core).
Axes of the slice: x: 4, y: 8, z: 8, core: 2. Of those that a mesh axis runs over, the one named last changes fastest.
Arguments:
- start_amps: bfloat16 [6, 1024, 2048], P(None, 'ch'), may hold values from -6 to 6
- energies: float32 [6], replicated, may hold values from 0.5 to 2
- thresholds: bfloat16 [32, 1024], P('sec', 'ch'), may hold values from -3 to -1
- intersection: bfloat16 [32, 1024, 1024], P('sec', 'ch'), may hold values from -0.2 to 1
Outputs:
- boundary_amps: bfloat16 [32, 6, 1024, 2048], P('sec', None, 'ch')
The draws below stay inside these ranges and needn't reach their ends.
All inputs are finite; a program needn't handle non-finite values.
Results may differ from the reference program's by a relative error of at most 0.04.
Values may be sent and summed in bfloat16 or wider, within the bound.
No kernel may reach another device: no remote copies, remote signals or barrier semaphores. Data moves between devices by JAX's collectives and lax.ppermute only.
A program may use at most 64 MiB of HBM per device.

```python
import math
import jax
import jax.numpy as jnp
from jax import lax

CH = 1024
NV = 1024
NE = 6
SECTORS = 32


def draw_intersection(key, part):
    spread = jax.random.truncated_normal(key, -4.0, 4.0, (SECTORS, CH, CH), jnp.float32) * (0.25 / math.sqrt(2.0 * CH))
    skewed = spread - jnp.swapaxes(spread, 1, 2)
    identity = jnp.eye(CH, dtype=jnp.float32)[None, :, :]
    return ((identity + skewed) / math.sqrt(1.0625)).astype(jnp.bfloat16)


def steps_of(key, extent, shards, low, largest):
    def one(axis_at, parts):
        draws = jax.random.uniform(jax.random.fold_in(jax.random.fold_in(key, 6), axis_at), (parts,), jnp.float32, low / len(shards), largest / len(shards))
        return jnp.repeat(jnp.exp(draws), extent[axis_at] // parts).reshape((-1,) + (1,) * (len(extent) - axis_at - 1))

    loudness = one(*shards[0])
    for cut in shards[1:]:
        loudness = loudness * one(*cut)
    return loudness


def scatter_about(rng, shape, scale, limit, cuts=(), kind=jnp.bfloat16):
    array = scale * jax.random.normal(rng, shape, jnp.float32)
    if cuts:
        array = array * steps_of(rng, shape, cuts, -0.22, 0.18)
    return jnp.clip(array, -limit, limit).astype(kind)


def setup_inputs(seed: int = 0) -> dict:
    keys = jax.random.split(jax.random.key(seed), 5)
    return {
        "start_amps": scatter_about(keys[0], (NE, CH, 2 * NV), 1.0, 6.0, ((1, 16),)),
        "energies": jnp.clip(jax.random.uniform(keys[1], (NE,), jnp.float32, 0.5, 2.0), 0.5, 2.0),
        "thresholds": jnp.clip(-3.0 + 2.0 * jax.random.uniform(keys[2], (SECTORS, CH), jnp.float32) ** steps_of(keys[2], (SECTORS, CH), ((0, 32), (1, 16)), -0.2, 0.2), -3.0, -1.0).astype(jnp.bfloat16),
        "intersection": draw_intersection(jax.random.fold_in(keys[4], 71), 0),
    }


def rotate(amplitude, wavenumber):
    half = amplitude.shape[-1] // 2
    values_part = amplitude[..., :half]
    slopes_part = amplitude[..., half:]
    cosine = jnp.cos(wavenumber)
    sine_term = jnp.sin(wavenumber)
    new_values = cosine * values_part + sine_term / wavenumber * slopes_part
    new_slopes = -wavenumber * sine_term * values_part + cosine * slopes_part
    return jnp.concatenate([new_values, new_slopes], axis=-1)

def reference(start_amps, energies, thresholds, intersection):

    def advance(amplitude, sector_data):
        channel_thresholds, basis_change = sector_data
        wavenumber = jnp.sqrt(energies[:, None] - channel_thresholds.astype(jnp.float32)[None, :])[:, :, None]
        rotated = rotate(amplitude, wavenumber).astype(jnp.bfloat16)
        product = jnp.einsum('ij,ejn->ein', basis_change.astype(jnp.float32), rotated.astype(jnp.float32))
        fresh = product.astype(jnp.bfloat16)
        return (fresh.astype(jnp.float32), fresh)
    initial = start_amps.astype(jnp.float32)
    final_state, boundary_amps = lax.scan(advance, initial, (thresholds, intersection))
    return boundary_amps
```

```python
import jax
import jax.numpy as jnp
from jax import lax
from jax.experimental import pallas as pl
from jax.experimental.pallas import tpu as pltpu
from jax.sharding import Mesh
from jax.sharding import PartitionSpec as P

AXES = ("y", "x", "z", "core")
SIZES = (8, 4, 8, 2)
CH_AXES = ("z", "core")
PLANE = ("x", "z", "core")
VMEM = 56 * 1024 * 1024


def spread_kernel(x_ref, v_ref, p_ref, out_ref):
    both = jnp.concatenate([v_ref[0], p_ref[0]], axis=0).astype(jnp.float32)
    turned = both.T.astype(jnp.bfloat16)
    groups, _, per, lanes = out_ref.shape
    out_ref[...] = turned.reshape(groups, 1, per, lanes)


def spread(x_index, start):
    energies, rows, width = start.shape
    cols = width // 8
    per = cols // 16
    return pl.pallas_call(
        spread_kernel,
        grid_spec=pltpu.PrefetchScalarGridSpec(
            num_scalar_prefetch=1,
            grid=(energies,),
            in_specs=[
                pl.BlockSpec((1, rows, cols), lambda e, x: (e, 0, x[0])),
                pl.BlockSpec((1, rows, cols), lambda e, x: (e, 0, 4 + x[0])),
            ],
            out_specs=pl.BlockSpec((16, 1, per, 2 * rows), lambda e, x: (0, e, 0, 0)),
        ),
        out_shape=jax.ShapeDtypeStruct((16, energies, per, 2 * rows), start.dtype),
        name="spread",
    )(x_index, start, start)


def join_kernel(in_ref, out_ref):
    rows = in_ref.shape[1]
    low = lax.broadcasted_iota(jnp.int32, (rows, 128), 1) < 64
    for z in range(8):
        one = in_ref[2 * z].astype(jnp.float32)
        two = in_ref[2 * z + 1].astype(jnp.float32)
        lanes = pl.ds(128 * z, 128)
        out_ref[0, :, lanes] = jnp.where(low, one, pltpu.roll(two, 64, 1)).astype(out_ref.dtype)
        out_ref[1, :, lanes] = jnp.where(low, pltpu.roll(one, 64, 1), two).astype(out_ref.dtype)


def join(pieces):
    rows = pieces.shape[1]
    return pl.pallas_call(
        join_kernel,
        out_shape=jax.ShapeDtypeStruct((2, rows, 1024), pieces.dtype),
        name="join",
    )(pieces)


def stage_kernel(active, state_ref, basis_ref, coef_ref, kept_ref, next_ref, out_ref, now, rot):
    del active, kept_ref
    s = pl.program_id(0)
    energies = coef_ref.shape[2]
    rows = state_ref.shape[1]
    per = rows // energies

    @pl.when(s == 0)
    def _():
        now[pl.ds(0, rows)] = state_ref[0]
        now[pl.ds(rows, rows)] = state_ref[1]

    for e in range(energies):
        cosine = coef_ref[0, 0, pl.ds(e, 1), :]
        ratio = coef_ref[0, 1, pl.ds(e, 1), :]
        product = coef_ref[0, 2, pl.ds(e, 1), :]
        values = now[pl.ds(per * e, per), :].astype(jnp.float32)
        slopes = now[pl.ds(rows + per * e, per), :].astype(jnp.float32)
        rot[pl.ds(per * e, per), :] = (cosine * values + ratio * slopes).astype(rot.dtype)
        rot[pl.ds(rows + per * e, per), :] = (cosine * slopes - product * values).astype(rot.dtype)
    fresh = lax.dot_general(
        rot[...], basis_ref[0], (((1,), (1,)), ((), ())), preferred_element_type=jnp.float32
    )
    rounded = fresh.astype(now.dtype)
    now[...] = rounded
    low = lax.broadcasted_iota(jnp.int32, (rows, 128), 1) < 64
    for z in range(8):
        lanes = slice(128 * z, 128 * z + 128)
        values = fresh[:rows, lanes]
        slopes = fresh[rows:, lanes]
        out_ref[0, 2 * z] = jnp.where(low, values, pltpu.roll(slopes, 64, 1)).astype(out_ref.dtype)
        out_ref[0, 2 * z + 1] = jnp.where(low, pltpu.roll(values, 64, 1), slopes).astype(out_ref.dtype)

    @pl.when(s == pl.num_programs(0) - 1)
    def _():
        next_ref[0] = rounded[:rows]
        next_ref[1] = rounded[rows:]


def stage(active, state, basis, coefs, kept):
    sectors, channels, _ = basis.shape
    rows = state.shape[1]
    return pl.pallas_call(
        stage_kernel,
        grid_spec=pltpu.PrefetchScalarGridSpec(
            num_scalar_prefetch=1,
            grid=(sectors,),
            in_specs=[
                pl.BlockSpec(state.shape, lambda s, a: (0, 0, 0)),
                pl.BlockSpec((1, channels, channels), lambda s, a: (s, 0, 0)),
                pl.BlockSpec((1,) + coefs.shape[1:], lambda s, a: (s, 0, 0, 0)),
                pl.BlockSpec(memory_space=pl.ANY),
            ],
            out_specs=[
                pl.BlockSpec(state.shape, lambda s, a: (0, 0, 0)),
                pl.BlockSpec((1, 16, rows, 128), lambda s, a: (jnp.where(a[0] == 1, s, sectors), 0, 0, 0)),
            ],
            scratch_shapes=[
                pltpu.VMEM((2 * rows, channels), state.dtype),
                pltpu.VMEM((2 * rows, channels), state.dtype),
            ],
        ),
        out_shape=[
            jax.ShapeDtypeStruct(state.shape, state.dtype),
            jax.ShapeDtypeStruct(kept.shape, kept.dtype),
        ],
        input_output_aliases={4: 1},
        compiler_params=pltpu.CompilerParams(vmem_limit_bytes=VMEM),
        name="stage",
    )(active, state, basis, coefs, kept)


def finish_kernel(in_ref, out_ref):
    groups, _, per, lanes = in_ref.shape
    turned = in_ref[...].reshape(groups * per, lanes).astype(jnp.float32).T.astype(out_ref.dtype)
    half = lanes // 2
    cols = groups * per
    out_ref[0, :, pl.ds(0, cols)] = turned[:half]
    out_ref[0, :, pl.ds(cols, cols)] = turned[half:]


def finish(pieces):
    groups, energies, per, lanes = pieces.shape
    return pl.pallas_call(
        finish_kernel,
        grid=(energies,),
        in_specs=[pl.BlockSpec((groups, 1, per, lanes), lambda e: (0, e, 0, 0))],
        out_specs=pl.BlockSpec((1, lanes // 2, 2 * groups * per), lambda e: (e, 0, 0)),
        out_shape=jax.ShapeDtypeStruct((energies, lanes // 2, 2 * groups * per), pieces.dtype),
        compiler_params=pltpu.CompilerParams(vmem_limit_bytes=VMEM),
        name="finish",
    )(pieces)


def per_device(start_amps, energies, thresholds, intersection):
    planes = lax.axis_size("y")
    y_index = lax.axis_index("y")
    x_index = lax.axis_index("x").astype(jnp.int32).reshape(1)
    count = energies.shape[0]
    channels = intersection.shape[2]
    basis = lax.all_gather(intersection[0], PLANE, tiled=True).reshape(4, channels, channels)
    limits = lax.all_gather(thresholds[0], PLANE, tiled=True).reshape(4, 1, channels)
    wave = jnp.sqrt(energies[None, :, None] - limits.astype(jnp.float32))
    sine = jnp.sin(wave)
    coefs = jnp.stack([jnp.cos(wave), sine / wave, wave * sine], axis=1)

    blocks = spread(x_index, start_amps)
    per, lanes = blocks.shape[2:]
    rows = count * per
    state = join(lax.all_to_all(blocks.reshape(16, rows, lanes), CH_AXES, 0, 0))
    kept = jnp.zeros((5, 16, rows, lanes), jnp.bfloat16)
    for step in range(planes):
        if step:
            state = lax.ppermute(state, "y", [(k, k + 1) for k in range(planes - 1)])
        active = (y_index == step).astype(jnp.int32).reshape(1)
        state, kept = stage(active, state, basis, coefs, kept)
    back = lax.all_to_all(kept[:4].reshape(64, rows, lanes), PLANE, 0, 0)
    return finish(back.reshape(64, count, per, lanes))[None]


def solution(mesh):
    fine = Mesh(mesh.devices.reshape(SIZES), AXES)
    sec, ch = ("y", "x"), CH_AXES
    in_specs = (P(None, ch, None), P(), P(sec, ch), P(sec, ch, None))
    out_specs = P(sec, None, ch, None)
    return jax.shard_map(
        per_device, mesh=fine, in_specs=in_specs, out_specs=out_specs, check_vma=False
    )
```

```python
import jax
import jax.numpy as jnp
from jax import lax
from jax.experimental import pallas as pl
from jax.experimental.pallas import tpu as pltpu
from jax.sharding import Mesh
from jax.sharding import PartitionSpec as P

AXES = ("y", "x", "z", "core")
SIZES = (8, 4, 8, 2)
CH_AXES = ("z", "core")
PLANE = ("x", "z", "core")
VMEM = 16 * 1024 * 1024


def spread_kernel(x_ref, v_ref, p_ref, limit_ref, out_ref):
    e = pl.program_id(0)
    both = jnp.concatenate([v_ref[0], p_ref[0]], axis=0).astype(jnp.float32)
    turned = both.T.astype(jnp.bfloat16)
    groups, _, per, lanes = out_ref.shape
    out_ref[...] = turned.reshape(groups, 1, per, lanes)

    @pl.when(e == pl.num_programs(0) - 1)
    def _():
        for k in range(groups):
            out_ref[k, 0] = limit_ref[...]


def spread(x_index, start, limits):
    energies, rows, width = start.shape
    cols = width // 8
    per = cols // 16
    return pl.pallas_call(
        spread_kernel,
        grid_spec=pltpu.PrefetchScalarGridSpec(
            num_scalar_prefetch=1,
            grid=(energies + 1,),
            in_specs=[
                pl.BlockSpec((1, rows, cols), lambda e, x: (jnp.minimum(e, energies - 1), 0, x[0])),
                pl.BlockSpec((1, rows, cols), lambda e, x: (jnp.minimum(e, energies - 1), 0, 4 + x[0])),
                pl.BlockSpec(limits.shape, lambda e, x: (0, 0)),
            ],
            out_specs=pl.BlockSpec((16, 1, per, 2 * rows), lambda e, x: (0, e, 0, 0)),
        ),
        out_shape=jax.ShapeDtypeStruct((16, energies + 1, per, 2 * rows), start.dtype),
        name="spread",
    )(x_index, start, start, limits)


def join_kernel(in_ref, out_ref):
    rows = out_ref.shape[1]
    low = lax.broadcasted_iota(jnp.int32, (rows, 128), 1) < 64
    for z in range(8):
        one = in_ref[2 * z, pl.ds(0, rows)].astype(jnp.float32)
        two = in_ref[2 * z + 1, pl.ds(0, rows)].astype(jnp.float32)
        lanes = pl.ds(128 * z, 128)
        out_ref[0, :, lanes] = jnp.where(low, one, pltpu.roll(two, 64, 1)).astype(out_ref.dtype)
        out_ref[1, :, lanes] = jnp.where(low, pltpu.roll(one, 64, 1), two).astype(out_ref.dtype)


def join(pieces, rows):
    return pl.pallas_call(
        join_kernel,
        out_shape=jax.ShapeDtypeStruct((2, rows, 1024), pieces.dtype),
        name="join",
    )(pieces)


def stage_kernel(active, state_ref, basis_ref, coef_ref, kept_ref, next_ref, out_ref, now, rot):
    del active, kept_ref
    s = pl.program_id(0)
    energies = coef_ref.shape[2]
    rows = state_ref.shape[1]
    per = rows // energies

    @pl.when(s == 0)
    def _():
        now[pl.ds(0, rows)] = state_ref[0]
        now[pl.ds(rows, rows)] = state_ref[1]

    for e in range(energies):
        cosine = coef_ref[0, 0, pl.ds(e, 1), :]
        ratio = coef_ref[0, 1, pl.ds(e, 1), :]
        product = coef_ref[0, 2, pl.ds(e, 1), :]
        values = now[pl.ds(per * e, per), :].astype(jnp.float32)
        slopes = now[pl.ds(rows + per * e, per), :].astype(jnp.float32)
        rot[pl.ds(per * e, per), :] = (cosine * values + ratio * slopes).astype(rot.dtype)
        rot[pl.ds(rows + per * e, per), :] = (cosine * slopes - product * values).astype(rot.dtype)
    channels = now.shape[1]
    fresh = lax.dot_general(
        rot[...],
        basis_ref[...].reshape(channels, channels),
        (((1,), (1,)), ((), ())),
        preferred_element_type=jnp.float32,
    )
    rounded = fresh.astype(now.dtype)
    now[...] = rounded
    low = lax.broadcasted_iota(jnp.int32, (rows, 128), 1) < 64
    for z in range(8):
        lanes = slice(128 * z, 128 * z + 128)
        values = fresh[:rows, lanes]
        slopes = fresh[rows:, lanes]
        out_ref[0, 2 * z] = jnp.where(low, values, pltpu.roll(slopes, 64, 1)).astype(out_ref.dtype)
        out_ref[0, 2 * z + 1] = jnp.where(low, pltpu.roll(values, 64, 1), slopes).astype(out_ref.dtype)

    @pl.when(s == pl.num_programs(0) - 1)
    def _():
        next_ref[0] = rounded[:rows]
        next_ref[1] = rounded[rows:]


def stage(active, state, basis, coefs, kept):
    groups, sectors, share, channels = basis.shape
    rows = state.shape[1]
    return pl.pallas_call(
        stage_kernel,
        grid_spec=pltpu.PrefetchScalarGridSpec(
            num_scalar_prefetch=1,
            grid=(sectors,),
            in_specs=[
                pl.BlockSpec(state.shape, lambda s, a: (0, 0, 0)),
                pl.BlockSpec((groups, 1, share, channels), lambda s, a: (0, s, 0, 0)),
                pl.BlockSpec((1,) + coefs.shape[1:], lambda s, a: (s, 0, 0, 0)),
                pl.BlockSpec(memory_space=pl.ANY),
            ],
            out_specs=[
                pl.BlockSpec(state.shape, lambda s, a: (0, 0, 0)),
                pl.BlockSpec((1, 16, rows, 128), lambda s, a: (jnp.where(a[0] == 1, s, sectors), 0, 0, 0)),
            ],
            scratch_shapes=[
                pltpu.VMEM((2 * rows, channels), state.dtype),
                pltpu.VMEM((2 * rows, channels), state.dtype),
            ],
        ),
        out_shape=[
            jax.ShapeDtypeStruct(state.shape, state.dtype),
            jax.ShapeDtypeStruct(kept.shape, kept.dtype),
        ],
        input_output_aliases={4: 1},
        compiler_params=pltpu.CompilerParams(vmem_limit_bytes=VMEM),
        name="stage",
    )(active, state, basis, coefs, kept)


def finish_kernel(in_ref, out_ref):
    groups, _, per, lanes = in_ref.shape
    turned = in_ref[...].reshape(groups * per, lanes).astype(jnp.float32).T.astype(out_ref.dtype)
    half = lanes // 2
    cols = groups * per
    out_ref[0, :, pl.ds(0, cols)] = turned[:half]
    out_ref[0, :, pl.ds(cols, cols)] = turned[half:]


def finish(pieces):
    groups, energies, per, lanes = pieces.shape
    return pl.pallas_call(
        finish_kernel,
        grid=(energies,),
        in_specs=[pl.BlockSpec((groups, 1, per, lanes), lambda e: (0, e, 0, 0))],
        out_specs=pl.BlockSpec((1, lanes // 2, 2 * groups * per), lambda e: (e, 0, 0)),
        out_shape=jax.ShapeDtypeStruct((energies, lanes // 2, 2 * groups * per), pieces.dtype),
        name="finish",
    )(pieces)


def per_device(start_amps, energies, thresholds, intersection):
    planes = lax.axis_size("y")
    y_index = lax.axis_index("y")
    x_index = lax.axis_index("x").astype(jnp.int32).reshape(1)
    count = energies.shape[0]
    channels = intersection.shape[2]
    share = intersection.shape[1]
    extra = jnp.pad(thresholds, ((0, 7), (0, channels - share)))
    ring = lax.all_gather(jnp.concatenate([intersection[0], extra]), "x")
    basis = lax.all_gather(ring[:, :share], CH_AXES)
    limits = jnp.pad(ring[:, share, :share].reshape(2, 2 * share), ((0, 14), (0, 0)))

    blocks = spread(x_index, start_amps, limits)
    per, lanes = blocks.shape[2:]
    rows = count * per
    blocks = lax.all_to_all(blocks.reshape(16, rows + per, lanes), CH_AXES, 0, 0)
    state = join(blocks, rows)
    limits = blocks[:, rows : rows + 2].reshape(16, 4, share).swapaxes(0, 1).reshape(4, 1, channels)
    wave = jnp.sqrt(energies[None, :, None] - limits.astype(jnp.float32))
    sine = jnp.sin(wave)
    coefs = jnp.stack([jnp.cos(wave), sine / wave, wave * sine], axis=1)
    kept = jnp.zeros((5, 16, rows, lanes), jnp.bfloat16)
    for step in range(planes):
        if step:
            state = lax.ppermute(state, "y", [(k, k + 1) for k in range(planes - 1)])
        active = (y_index == step).astype(jnp.int32).reshape(1)
        state, kept = stage(active, state, basis, coefs, kept)
    back = lax.all_to_all(kept[:4].reshape(64, rows, lanes), PLANE, 0, 0)
    return finish(back.reshape(64, count, per, lanes))[None]


def solution(mesh):
    fine = Mesh(mesh.devices.reshape(SIZES), AXES)
    sec, ch = ("y", "x"), CH_AXES
    in_specs = (P(None, ch, None), P(), P(sec, ch), P(sec, ch, None))
    out_specs = P(sec, None, ch, None)
    return jax.shard_map(
        per_device, mesh=fine, in_specs=in_specs, out_specs=out_specs, check_vma=False
    )
```

```python
import jax
import jax.numpy as jnp
from jax import lax
from jax.experimental import pallas as pl
from jax.experimental.pallas import tpu as pltpu
from jax.sharding import Mesh
from jax.sharding import PartitionSpec as P

AXES = ("y", "x", "z", "core")
SIZES = (8, 4, 8, 2)
CH_AXES = ("z", "core")
PLANE = ("x", "z", "core")
MIB = 1024 * 1024


def spread_kernel(x_ref, v_ref, p_ref, limit_ref, out_ref):
    e = pl.program_id(0)
    both = jnp.concatenate([v_ref[0], p_ref[0]], axis=0).astype(jnp.float32)
    turned = both.T.astype(jnp.bfloat16)
    groups, _, per, lanes = out_ref.shape
    out_ref[...] = turned.reshape(groups, 1, per, lanes)

    @pl.when(e == pl.num_programs(0) - 1)
    def _():
        for k in range(groups):
            out_ref[k, 0] = limit_ref[...]


def spread(x_index, start, limits):
    energies, rows, width = start.shape
    cols = width // 8
    per = cols // 16
    return pl.pallas_call(
        spread_kernel,
        grid_spec=pltpu.PrefetchScalarGridSpec(
            num_scalar_prefetch=1,
            grid=(energies + 1,),
            in_specs=[
                pl.BlockSpec((1, rows, cols), lambda e, x: (jnp.minimum(e, energies - 1), 0, x[0])),
                pl.BlockSpec((1, rows, cols), lambda e, x: (jnp.minimum(e, energies - 1), 0, 4 + x[0])),
                pl.BlockSpec(limits.shape, lambda e, x: (0, 0)),
            ],
            out_specs=pl.BlockSpec((16, 1, per, 2 * rows), lambda e, x: (0, e, 0, 0)),
        ),
        out_shape=jax.ShapeDtypeStruct((16, energies + 1, per, 2 * rows), start.dtype),
        name="spread",
    )(x_index, start, start, limits)


def join_kernel(in_ref, out_ref):
    rows = out_ref.shape[1]
    low = lax.broadcasted_iota(jnp.int32, (rows, 128), 1) < 64
    for z in range(8):
        one = in_ref[2 * z, pl.ds(0, rows)].astype(jnp.float32)
        two = in_ref[2 * z + 1, pl.ds(0, rows)].astype(jnp.float32)
        lanes = pl.ds(128 * z, 128)
        out_ref[0, :, lanes] = jnp.where(low, one, pltpu.roll(two, 64, 1)).astype(out_ref.dtype)
        out_ref[1, :, lanes] = jnp.where(low, pltpu.roll(one, 64, 1), two).astype(out_ref.dtype)


def join(pieces, rows):
    return pl.pallas_call(
        join_kernel,
        out_shape=jax.ShapeDtypeStruct((2, rows, 1024), pieces.dtype),
        name="join",
    )(pieces)


def turn_kernel(*refs):
    out_ref = refs[-1]
    for q, ref in enumerate(refs[:-1]):
        groups, _, share, channels = ref.shape
        block = ref[...].reshape(groups * share, channels)
        out_ref[0, :, pl.ds(groups * share * q, groups * share)] = block.T


def turn(basis):
    groups, sectors, share, channels = basis.shape
    part = groups // 4
    specs = [pl.BlockSpec((part, 1, share, channels), lambda s, q=q: (q, s, 0, 0)) for q in range(4)]
    return pl.pallas_call(
        turn_kernel,
        grid=(sectors,),
        in_specs=specs,
        out_specs=pl.BlockSpec((1, channels, groups * share), lambda s: (s, 0, 0)),
        out_shape=jax.ShapeDtypeStruct((sectors, channels, groups * share), basis.dtype),
        compiler_params=pltpu.CompilerParams(vmem_limit_bytes=40 * MIB),
        name="turn",
    )(basis, basis, basis, basis)


def stage_kernel(y_ref, state_ref, basis_ref, coef_ref, *refs):
    next_ref, out_ref, now, rot = refs[-4:]
    del y_ref
    s = pl.program_id(0)
    energies = coef_ref.shape[2]
    rows = state_ref.shape[1]
    per = rows // energies

    @pl.when(s == 0)
    def _():
        now[pl.ds(0, rows)] = state_ref[0]
        now[pl.ds(rows, rows)] = state_ref[1]

    for e in range(energies):
        cosine = coef_ref[0, 0, pl.ds(e, 1), :]
        ratio = coef_ref[0, 1, pl.ds(e, 1), :]
        product = coef_ref[0, 2, pl.ds(e, 1), :]
        values = now[pl.ds(per * e, per), :].astype(jnp.float32)
        slopes = now[pl.ds(rows + per * e, per), :].astype(jnp.float32)
        rot[pl.ds(per * e, per), :] = (cosine * values + ratio * slopes).astype(rot.dtype)
        rot[pl.ds(rows + per * e, per), :] = (cosine * slopes - product * values).astype(rot.dtype)
    fresh = jnp.dot(rot[...], basis_ref[0], preferred_element_type=jnp.float32)
    rounded = fresh.astype(now.dtype)
    now[...] = rounded
    low = lax.broadcasted_iota(jnp.int32, (rows, 128), 1) < 64
    for z in range(8):
        lanes = slice(128 * z, 128 * z + 128)
        values = fresh[:rows, lanes]
        slopes = fresh[rows:, lanes]
        out_ref[0, 2 * z] = jnp.where(low, values, pltpu.roll(slopes, 64, 1)).astype(out_ref.dtype)
        out_ref[0, 2 * z + 1] = jnp.where(low, pltpu.roll(values, 64, 1), slopes).astype(out_ref.dtype)

    @pl.when(s == pl.num_programs(0) - 1)
    def _():
        next_ref[0] = rounded[:rows]
        next_ref[1] = rounded[rows:]


def stage(step, y_index, state, basis, coefs, kept):
    sectors, channels, _ = basis.shape
    rows = state.shape[1]
    first = kept is None
    return pl.pallas_call(
        stage_kernel,
        grid_spec=pltpu.PrefetchScalarGridSpec(
            num_scalar_prefetch=1,
            grid=(sectors,),
            in_specs=[
                pl.BlockSpec(state.shape, lambda s, y: (0, 0, 0)),
                pl.BlockSpec((1, channels, channels), lambda s, y: (s, 0, 0)),
                pl.BlockSpec((1,) + coefs.shape[1:], lambda s, y: (s, 0, 0, 0)),
            ]
            + ([] if first else [pl.BlockSpec(memory_space=pl.ANY)]),
            out_specs=[
                pl.BlockSpec(state.shape, lambda s, y: (0, 0, 0)),
                pl.BlockSpec((1, 16, rows, 128), lambda s, y: (jnp.where(y[0] == step, s, sectors), 0, 0, 0)),
            ],
            scratch_shapes=[
                pltpu.VMEM((2 * rows, channels), state.dtype),
                pltpu.VMEM((2 * rows, channels), state.dtype),
            ],
        ),
        out_shape=[
            jax.ShapeDtypeStruct(state.shape, state.dtype),
            jax.ShapeDtypeStruct((sectors + 1, 16, rows, 128), state.dtype),
        ],
        input_output_aliases={} if first else {4: 1},
        compiler_params=pltpu.CompilerParams(vmem_limit_bytes=16 * MIB),
        name="stage",
    )(y_index, state, basis, coefs, *([] if first else [kept]))


def finish_kernel(in_ref, out_ref):
    groups, energies, per, lanes = in_ref.shape
    half = lanes // 2
    cols = groups * per
    for e in range(energies):
        turned = in_ref[:, e].reshape(cols, lanes).T
        out_ref[e, :, pl.ds(0, cols)] = turned[:half]
        out_ref[e, :, pl.ds(cols, cols)] = turned[half:]


def finish(pieces):
    groups, energies, per, lanes = pieces.shape
    batch = 2
    return pl.pallas_call(
        finish_kernel,
        grid=(energies // batch,),
        in_specs=[pl.BlockSpec((groups, batch, per, lanes), lambda e: (0, e, 0, 0))],
        out_specs=pl.BlockSpec((batch, lanes // 2, 2 * groups * per), lambda e: (e, 0, 0)),
        out_shape=jax.ShapeDtypeStruct((energies, lanes // 2, 2 * groups * per), pieces.dtype),
        compiler_params=pltpu.CompilerParams(vmem_limit_bytes=16 * MIB),
        name="finish",
    )(pieces)


def per_device(start_amps, energies, thresholds, intersection):
    planes = lax.axis_size("y")
    y_index = lax.axis_index("y").astype(jnp.int32).reshape(1)
    x_index = lax.axis_index("x").astype(jnp.int32).reshape(1)
    count = energies.shape[0]
    channels = intersection.shape[2]
    share = intersection.shape[1]
    extra = jnp.pad(thresholds, ((0, 7), (0, channels - share)))
    ring = lax.all_gather(jnp.concatenate([intersection[0], extra]), "x")
    basis = turn(lax.all_gather(ring[:, :share], CH_AXES))
    limits = jnp.pad(ring[:, share, :share].reshape(2, 2 * share), ((0, 14), (0, 0)))

    blocks = spread(x_index, start_amps, limits)
    per, lanes = blocks.shape[2:]
    rows = count * per
    blocks = lax.all_to_all(blocks.reshape(16, rows + per, lanes), CH_AXES, 0, 0)
    state = join(blocks, rows)
    limits = blocks[:, rows : rows + 2].reshape(16, 4, share).swapaxes(0, 1).reshape(4, 1, channels)
    wave = jnp.sqrt(energies[None, :, None] - limits.astype(jnp.float32))
    sine = jnp.sin(wave)
    coefs = jnp.stack([jnp.cos(wave), sine / wave, wave * sine], axis=1)
    kept = None
    for step in range(planes):
        if step:
            state = lax.ppermute(state, "y", [(k, k + 1) for k in range(planes - 1)])
        state, kept = stage(step, y_index, state, basis, coefs, kept)
    back = lax.all_to_all(kept[:4].reshape(64, rows, lanes), PLANE, 0, 0)
    return finish(back.reshape(64, count, per, lanes))[None]


def solution(mesh):
    fine = Mesh(mesh.devices.reshape(SIZES), AXES)
    sec, ch = ("y", "x"), CH_AXES
    in_specs = (P(None, ch, None), P(), P(sec, ch), P(sec, ch, None))
    out_specs = P(sec, None, ch, None)
    return jax.shard_map(
        per_device, mesh=fine, in_specs=in_specs, out_specs=out_specs, check_vma=False
    )
```

```python
import functools

import jax
import jax.numpy as jnp
from jax import lax
from jax.experimental import pallas as pl
from jax.experimental.pallas import tpu as pltpu
from jax.sharding import Mesh
from jax.sharding import PartitionSpec as P

AXES = ("y", "x", "z", "core")
SIZES = (8, 4, 8, 2)
CH_AXES = ("z", "core")
PLANE = ("x", "z", "core")
MIB = 1024 * 1024


def spread_kernel(x_ref, v_ref, p_ref, limit_ref, out_ref):
    e = pl.program_id(0)
    both = jnp.concatenate([v_ref[0], p_ref[0]], axis=0).astype(jnp.float32)
    turned = both.T.astype(jnp.bfloat16)
    groups, _, per, lanes = out_ref.shape
    out_ref[...] = turned.reshape(groups, 1, per, lanes)

    @pl.when(e == pl.num_programs(0) - 1)
    def _():
        for k in range(groups):
            out_ref[k, 0] = limit_ref[...]


def spread(x_index, start, limits):
    energies, rows, width = start.shape
    cols = width // 8
    per = cols // 16
    return pl.pallas_call(
        spread_kernel,
        grid_spec=pltpu.PrefetchScalarGridSpec(
            num_scalar_prefetch=1,
            grid=(energies + 1,),
            in_specs=[
                pl.BlockSpec((1, rows, cols), lambda e, x: (jnp.minimum(e, energies - 1), 0, x[0])),
                pl.BlockSpec((1, rows, cols), lambda e, x: (jnp.minimum(e, energies - 1), 0, 4 + x[0])),
                pl.BlockSpec(limits.shape, lambda e, x: (0, 0)),
            ],
            out_specs=pl.BlockSpec((16, 1, per, 2 * rows), lambda e, x: (0, e, 0, 0)),
        ),
        out_shape=jax.ShapeDtypeStruct((16, energies + 1, per, 2 * rows), start.dtype),
        name="spread",
    )(x_index, start, start, limits)


def join_kernel(in_ref, out_ref):
    rows = out_ref.shape[1]
    low = lax.broadcasted_iota(jnp.int32, (rows, 128), 1) < 64
    for z in range(8):
        one = in_ref[2 * z, pl.ds(0, rows)].astype(jnp.float32)
        two = in_ref[2 * z + 1, pl.ds(0, rows)].astype(jnp.float32)
        lanes = pl.ds(128 * z, 128)
        out_ref[0, :, lanes] = jnp.where(low, one, pltpu.roll(two, 64, 1)).astype(out_ref.dtype)
        out_ref[1, :, lanes] = jnp.where(low, pltpu.roll(one, 64, 1), two).astype(out_ref.dtype)


def join(pieces, rows):
    return pl.pallas_call(
        join_kernel,
        out_shape=jax.ShapeDtypeStruct((2, rows, 1024), pieces.dtype),
        name="join",
    )(pieces)


def turn_kernel(*refs):
    out_ref = refs[-1]
    for q, ref in enumerate(refs[:-1]):
        groups, _, share, channels = ref.shape
        block = ref[...].reshape(groups * share, channels)
        out_ref[0, :, pl.ds(groups * share * q, groups * share)] = block.T


def turn(basis):
    groups, sectors, share, channels = basis.shape
    part = groups // 4
    specs = [pl.BlockSpec((part, 1, share, channels), lambda s, q=q: (q, s, 0, 0)) for q in range(4)]
    return pl.pallas_call(
        turn_kernel,
        grid=(sectors,),
        in_specs=specs,
        out_specs=pl.BlockSpec((1, channels, groups * share), lambda s: (s, 0, 0)),
        out_shape=jax.ShapeDtypeStruct((sectors, channels, groups * share), basis.dtype),
        compiler_params=pltpu.CompilerParams(vmem_limit_bytes=40 * MIB),
        name="turn",
    )(basis, basis, basis, basis)


def stage_kernel(parts, y_ref, state_ref, *refs):
    basis_refs, coef_ref = refs[:parts], refs[parts]
    next_ref, out_ref, now, rot = refs[-4:]
    del y_ref
    s = pl.program_id(0)
    energies = coef_ref.shape[2]
    rows, channels = state_ref.shape[1:]
    per = rows // energies

    @pl.when(s == 0)
    def _():
        now[pl.ds(0, rows)] = state_ref[0]
        now[pl.ds(rows, rows)] = state_ref[1]

    for e in range(energies):
        cosine = coef_ref[0, 0, pl.ds(e, 1), :]
        ratio = coef_ref[0, 1, pl.ds(e, 1), :]
        product = coef_ref[0, 2, pl.ds(e, 1), :]
        values = now[pl.ds(per * e, per), :].astype(jnp.float32)
        slopes = now[pl.ds(rows + per * e, per), :].astype(jnp.float32)
        rot[pl.ds(per * e, per), :] = (cosine * values + ratio * slopes).astype(rot.dtype)
        rot[pl.ds(rows + per * e, per), :] = (cosine * slopes - product * values).astype(rot.dtype)
    low = lax.broadcasted_iota(jnp.int32, (rows, 128), 1) < 64
    width = channels // parts
    for q, basis_ref in enumerate(basis_refs):
        if parts == 1:
            fresh = jnp.dot(rot[...], basis_ref[0], preferred_element_type=jnp.float32)
        else:
            block = basis_ref[...].reshape(width, channels)
            fresh = lax.dot_general(
                rot[...], block, (((1,), (1,)), ((), ())), preferred_element_type=jnp.float32
            )
        now[:, pl.ds(width * q, width)] = fresh.astype(now.dtype)
        for k in range(width // 128):
            z = width // 128 * q + k
            lanes = slice(128 * k, 128 * k + 128)
            values = fresh[:rows, lanes]
            slopes = fresh[rows:, lanes]
            out_ref[0, 2 * z] = jnp.where(low, values, pltpu.roll(slopes, 64, 1)).astype(out_ref.dtype)
            out_ref[0, 2 * z + 1] = jnp.where(low, pltpu.roll(values, 64, 1), slopes).astype(out_ref.dtype)

    @pl.when(s == pl.num_programs(0) - 1)
    def _():
        next_ref[0] = now[pl.ds(0, rows)]
        next_ref[1] = now[pl.ds(rows, rows)]


def stage(step, y_index, state, basis, coefs, kept):
    sectors = coefs.shape[0]
    _, rows, channels = state.shape
    first = kept is None
    parts = 4 if first else 1
    if first:
        groups, _, share, _ = basis.shape
        block = (groups // parts, 1, share, channels)
        basis_specs = [pl.BlockSpec(block, lambda s, y, q=q: (q, s, 0, 0)) for q in range(parts)]
    else:
        basis_specs = [pl.BlockSpec((1, channels, channels), lambda s, y: (s, 0, 0))]
    return pl.pallas_call(
        functools.partial(stage_kernel, parts),
        grid_spec=pltpu.PrefetchScalarGridSpec(
            num_scalar_prefetch=1,
            grid=(sectors,),
            in_specs=[pl.BlockSpec(state.shape, lambda s, y: (0, 0, 0))]
            + basis_specs
            + [pl.BlockSpec((1,) + coefs.shape[1:], lambda s, y: (s, 0, 0, 0))]
            + ([] if first else [pl.BlockSpec(memory_space=pl.ANY)]),
            out_specs=[
                pl.BlockSpec(state.shape, lambda s, y: (0, 0, 0)),
                pl.BlockSpec((1, 16, rows, 128), lambda s, y: (jnp.where(y[0] == step, s, sectors), 0, 0, 0)),
            ],
            scratch_shapes=[
                pltpu.VMEM((2 * rows, channels), state.dtype),
                pltpu.VMEM((2 * rows, channels), state.dtype),
            ],
        ),
        out_shape=[
            jax.ShapeDtypeStruct(state.shape, state.dtype),
            jax.ShapeDtypeStruct((sectors + 1, 16, rows, 128), state.dtype),
        ],
        input_output_aliases={} if first else {4: 1},
        compiler_params=pltpu.CompilerParams(vmem_limit_bytes=(48 if first else 16) * MIB),
        name="stage",
    )(y_index, state, *[basis] * parts, coefs, *([] if first else [kept]))


def finish_kernel(in_ref, out_ref):
    groups, energies, per, lanes = in_ref.shape
    half = lanes // 2
    cols = groups * per
    for e in range(energies):
        turned = in_ref[:, e].reshape(cols, lanes).T
        out_ref[e, :, pl.ds(0, cols)] = turned[:half]
        out_ref[e, :, pl.ds(cols, cols)] = turned[half:]


def finish(pieces):
    groups, energies, per, lanes = pieces.shape
    batch = 2
    return pl.pallas_call(
        finish_kernel,
        grid=(energies // batch,),
        in_specs=[pl.BlockSpec((groups, batch, per, lanes), lambda e: (0, e, 0, 0))],
        out_specs=pl.BlockSpec((batch, lanes // 2, 2 * groups * per), lambda e: (e, 0, 0)),
        out_shape=jax.ShapeDtypeStruct((energies, lanes // 2, 2 * groups * per), pieces.dtype),
        compiler_params=pltpu.CompilerParams(vmem_limit_bytes=16 * MIB),
        name="finish",
    )(pieces)


def per_device(start_amps, energies, thresholds, intersection):
    planes = lax.axis_size("y")
    y_index = lax.axis_index("y").astype(jnp.int32).reshape(1)
    x_index = lax.axis_index("x").astype(jnp.int32).reshape(1)
    count = energies.shape[0]
    channels = intersection.shape[2]
    share = intersection.shape[1]
    extra = jnp.pad(thresholds, ((0, 7), (0, channels - share)))
    ring = lax.all_gather(jnp.concatenate([intersection[0], extra]), "x")
    basis = lax.all_gather(ring[:, :share], CH_AXES)
    limits = jnp.pad(ring[:, share, :share].reshape(2, 2 * share), ((0, 14), (0, 0)))

    blocks = spread(x_index, start_amps, limits)
    per, lanes = blocks.shape[2:]
    rows = count * per
    blocks = lax.all_to_all(blocks.reshape(16, rows + per, lanes), CH_AXES, 0, 0)
    state = join(blocks, rows)
    limits = blocks[:, rows : rows + 2].reshape(16, 4, share).swapaxes(0, 1).reshape(4, 1, channels)
    wave = jnp.sqrt(energies[None, :, None] - limits.astype(jnp.float32))
    sine = jnp.sin(wave)
    coefs = jnp.stack([jnp.cos(wave), sine / wave, wave * sine], axis=1)
    kept = None
    for step in range(planes):
        if step:
            state = lax.ppermute(state, "y", [(step - 1, step)])
        if step == 1:
            basis = turn(basis)
        state, kept = stage(step, y_index, state, basis, coefs, kept)
    back = lax.all_to_all(kept[:4].reshape(64, rows, lanes), PLANE, 0, 0)
    return finish(back.reshape(64, count, per, lanes))[None]


def solution(mesh):
    fine = Mesh(mesh.devices.reshape(SIZES), AXES)
    sec, ch = ("y", "x"), CH_AXES
    in_specs = (P(None, ch, None), P(), P(sec, ch), P(sec, ch, None))
    out_specs = P(sec, None, ch, None)
    return jax.shard_map(
        per_device, mesh=fine, in_specs=in_specs, out_specs=out_specs, check_vma=False
    )
```

```python
import functools

import jax
import jax.numpy as jnp
from jax import lax
from jax.experimental import pallas as pl
from jax.experimental.pallas import tpu as pltpu
from jax.sharding import Mesh
from jax.sharding import PartitionSpec as P

AXES = ("y", "x", "z", "core")
SIZES = (8, 4, 8, 2)
CH_AXES = ("z", "core")
PLANE = ("x", "z", "core")
MIB = 1024 * 1024
PARTS = 2


def spread_kernel(x_ref, v_ref, p_ref, limit_ref, out_ref):
    e = pl.program_id(0)
    both = jnp.concatenate([v_ref[0], p_ref[0]], axis=0).astype(jnp.float32)
    turned = both.T.astype(jnp.bfloat16)
    groups, _, per, lanes = out_ref.shape
    out_ref[...] = turned.reshape(groups, 1, per, lanes)

    @pl.when(e == pl.num_programs(0) - 1)
    def _():
        for k in range(groups):
            out_ref[k, 0] = limit_ref[...]


def spread(x_index, start, limits):
    energies, rows, width = start.shape
    cols = width // 8
    per = cols // 16
    return pl.pallas_call(
        spread_kernel,
        grid_spec=pltpu.PrefetchScalarGridSpec(
            num_scalar_prefetch=1,
            grid=(energies + 1,),
            in_specs=[
                pl.BlockSpec((1, rows, cols), lambda e, x: (jnp.minimum(e, energies - 1), 0, x[0])),
                pl.BlockSpec((1, rows, cols), lambda e, x: (jnp.minimum(e, energies - 1), 0, 4 + x[0])),
                pl.BlockSpec(limits.shape, lambda e, x: (0, 0)),
            ],
            out_specs=pl.BlockSpec((16, 1, per, 2 * rows), lambda e, x: (0, e, 0, 0)),
        ),
        out_shape=jax.ShapeDtypeStruct((16, energies + 1, per, 2 * rows), start.dtype),
        name="spread",
    )(x_index, start, start, limits)


def join_kernel(in_ref, out_ref):
    rows = out_ref.shape[1]
    low = lax.broadcasted_iota(jnp.int32, (rows, 128), 1) < 64
    for z in range(8):
        one = in_ref[2 * z, pl.ds(0, rows)].astype(jnp.float32)
        two = in_ref[2 * z + 1, pl.ds(0, rows)].astype(jnp.float32)
        lanes = pl.ds(128 * z, 128)
        out_ref[0, :, lanes] = jnp.where(low, one, pltpu.roll(two, 64, 1)).astype(out_ref.dtype)
        out_ref[1, :, lanes] = jnp.where(low, pltpu.roll(one, 64, 1), two).astype(out_ref.dtype)


def join(pieces, rows):
    return pl.pallas_call(
        join_kernel,
        out_shape=jax.ShapeDtypeStruct((2, rows, 1024), pieces.dtype),
        name="join",
    )(pieces)


def turn_kernel(*refs):
    out_ref = refs[-1]
    for q, ref in enumerate(refs[:-1]):
        groups, _, share, channels = ref.shape
        block = ref[...].reshape(groups * share, channels)
        out_ref[0, :, pl.ds(groups * share * q, groups * share)] = block.T


def turn(basis):
    groups, sectors, share, channels = basis.shape
    part = groups // 4
    specs = [pl.BlockSpec((part, 1, share, channels), lambda s, q=q: (q, s, 0, 0)) for q in range(4)]
    return pl.pallas_call(
        turn_kernel,
        grid=(sectors,),
        in_specs=specs,
        out_specs=pl.BlockSpec((1, channels, groups * share), lambda s: (s, 0, 0)),
        out_shape=jax.ShapeDtypeStruct((sectors, channels, groups * share), basis.dtype),
        compiler_params=pltpu.CompilerParams(vmem_limit_bytes=40 * MIB),
        name="turn",
    )(basis, basis, basis, basis)


def stage_kernel(pieces, parts, y_ref, state_ref, *refs):
    basis_refs, coef_ref = refs[:pieces], refs[pieces]
    next_refs, (out_ref, now, rot) = refs[-3 - parts : -3], refs[-3:]
    del y_ref
    s = pl.program_id(0)
    energies = coef_ref.shape[3]
    rows, channels = state_ref.shape[1:]
    own = rows // parts
    per = own // energies

    @pl.when(s == 0)
    def _():
        now[pl.ds(0, rows)] = state_ref[0]
        now[pl.ds(rows, rows)] = state_ref[1]

    for k in range(parts * energies):
        part, e = divmod(k, energies)
        cosine = coef_ref[part, 0, 0, pl.ds(e, 1), :]
        ratio = coef_ref[part, 0, 1, pl.ds(e, 1), :]
        product = coef_ref[part, 0, 2, pl.ds(e, 1), :]
        values = now[pl.ds(per * k, per), :].astype(jnp.float32)
        slopes = now[pl.ds(rows + per * k, per), :].astype(jnp.float32)
        rot[pl.ds(per * k, per), :] = (cosine * values + ratio * slopes).astype(rot.dtype)
        rot[pl.ds(rows + per * k, per), :] = (cosine * slopes - product * values).astype(rot.dtype)
    low = lax.broadcasted_iota(jnp.int32, (rows, 128), 1) < 64
    width = channels // pieces
    for q, basis_ref in enumerate(basis_refs):
        if pieces == 1:
            fresh = jnp.dot(rot[...], basis_ref[0], preferred_element_type=jnp.float32)
        else:
            block = basis_ref[...].reshape(width, channels)
            fresh = lax.dot_general(
                rot[...], block, (((1,), (1,)), ((), ())), preferred_element_type=jnp.float32
            )
        now[:, pl.ds(width * q, width)] = fresh.astype(now.dtype)
        for k in range(width // 128):
            z = width // 128 * q + k
            lanes = slice(128 * k, 128 * k + 128)
            values = fresh[:rows, lanes]
            slopes = fresh[rows:, lanes]
            one = jnp.where(low, values, pltpu.roll(slopes, 64, 1)).astype(out_ref.dtype)
            two = jnp.where(low, pltpu.roll(values, 64, 1), slopes).astype(out_ref.dtype)
            out_ref[0, 2 * z] = one.reshape(parts, own, 128)
            out_ref[0, 2 * z + 1] = two.reshape(parts, own, 128)

    @pl.when(s == pl.num_programs(0) - 1)
    def _():
        for part, next_ref in enumerate(next_refs):
            next_ref[0] = now[pl.ds(own * part, own)]
            next_ref[1] = now[pl.ds(rows + own * part, own)]


def stage(step, part, y_index, state, basis, coefs, kept):
    sectors = coefs.shape[1]
    _, rows, channels = state.shape
    first = step == 0
    pieces, parts = (4, PARTS) if first else (1, 1)
    own = rows // parts
    if first:
        groups, _, share, _ = basis.shape
        block = (groups // pieces, 1, share, channels)
        basis_specs = [pl.BlockSpec(block, lambda s, y, q=q: (q, s, 0, 0)) for q in range(pieces)]
    else:
        basis_specs = [pl.BlockSpec((1, channels, channels), lambda s, y: (s, 0, 0))]
    outs = pl.pallas_call(
        functools.partial(stage_kernel, pieces, parts),
        grid_spec=pltpu.PrefetchScalarGridSpec(
            num_scalar_prefetch=1,
            grid=(sectors,),
            in_specs=[pl.BlockSpec(state.shape, lambda s, y: (0, 0, 0))]
            + basis_specs
            + [pl.BlockSpec((parts, 1) + coefs.shape[2:], lambda s, y: (part, s, 0, 0, 0))]
            + ([] if first else [pl.BlockSpec(memory_space=pl.ANY)]),
            out_specs=[pl.BlockSpec((2, own, channels), lambda s, y: (0, 0, 0))] * parts
            + [
                pl.BlockSpec(
                    (1, 16, parts, own, 128),
                    lambda s, y: (jnp.where(y[0] == step, s, sectors), 0, part, 0, 0),
                ),
            ],
            scratch_shapes=[
                pltpu.VMEM((2 * rows, channels), state.dtype),
                pltpu.VMEM((2 * rows, channels), state.dtype),
            ],
        ),
        out_shape=[jax.ShapeDtypeStruct((2, own, channels), state.dtype)] * parts
        + [jax.ShapeDtypeStruct((sectors + 1, 16, PARTS, own, 128), state.dtype)],
        input_output_aliases={} if first else {4: 1},
        compiler_params=pltpu.CompilerParams(vmem_limit_bytes=(48 if first else 16) * MIB),
        name="stage",
    )(y_index, state, *[basis] * pieces, coefs, *([] if first else [kept]))
    return list(outs[:-1]), outs[-1]


def finish_kernel(in_ref, out_ref):
    groups, energies, per, lanes = in_ref.shape
    half = lanes // 2
    cols = groups * per
    for e in range(energies):
        turned = in_ref[:, e].reshape(cols, lanes).T
        out_ref[e, :, pl.ds(0, cols)] = turned[:half]
        out_ref[e, :, pl.ds(cols, cols)] = turned[half:]


def finish(pieces):
    groups, energies, per, lanes = pieces.shape
    batch = 2
    return pl.pallas_call(
        finish_kernel,
        grid=(energies // batch,),
        in_specs=[pl.BlockSpec((groups, batch, per, lanes), lambda e: (0, e, 0, 0))],
        out_specs=pl.BlockSpec((batch, lanes // 2, 2 * groups * per), lambda e: (e, 0, 0)),
        out_shape=jax.ShapeDtypeStruct((energies, lanes // 2, 2 * groups * per), pieces.dtype),
        compiler_params=pltpu.CompilerParams(vmem_limit_bytes=16 * MIB),
        name="finish",
    )(pieces)


def per_device(start_amps, energies, thresholds, intersection):
    planes = lax.axis_size("y")
    y_index = lax.axis_index("y").astype(jnp.int32).reshape(1)
    x_index = lax.axis_index("x").astype(jnp.int32).reshape(1)
    count = energies.shape[0]
    channels = intersection.shape[2]
    share = intersection.shape[1]
    extra = jnp.pad(thresholds, ((0, 7), (0, channels - share)))
    ring = lax.all_gather(jnp.concatenate([intersection[0], extra]), "x")
    basis = lax.all_gather(ring[:, :share], CH_AXES)
    limits = jnp.pad(ring[:, share, :share].reshape(2, 2 * share), ((0, 14), (0, 0)))

    blocks = spread(x_index, start_amps, limits)
    per, lanes = blocks.shape[2:]
    rows = count * per
    blocks = lax.all_to_all(blocks.reshape(16, rows + per, lanes), CH_AXES, 0, 0)
    state = join(blocks, rows)
    limits = blocks[:, rows : rows + 2].reshape(16, 4, share).swapaxes(0, 1).reshape(4, 1, channels)
    wave = jnp.sqrt(energies[None, :, None] - limits.astype(jnp.float32))
    sine = jnp.sin(wave)
    coefs = jnp.stack([jnp.cos(wave), sine / wave, wave * sine], axis=1)
    coefs = coefs.reshape(4, 3, PARTS, count // PARTS, channels).transpose(2, 0, 1, 3, 4)
    states, kept = stage(0, 0, y_index, state, basis, coefs, None)
    basis = turn(basis)
    for step in range(1, planes):
        for part in range(PARTS):
            state = lax.ppermute(states[part], "y", [(step - 1, step)])
            (states[part],), kept = stage(step, part, y_index, state, basis, coefs, kept)
    back = lax.all_to_all(kept[:4].reshape(64, rows, lanes), PLANE, 0, 0)
    return finish(back.reshape(64, count, per, lanes))[None]


def solution(mesh):
    fine = Mesh(mesh.devices.reshape(SIZES), AXES)
    sec, ch = ("y", "x"), CH_AXES
    in_specs = (P(None, ch, None), P(), P(sec, ch), P(sec, ch, None))
    out_specs = P(sec, None, ch, None)
    return jax.shard_map(
        per_device, mesh=fine, in_specs=in_specs, out_specs=out_specs, check_vma=False
    )
```

```python
import functools

import jax
import jax.numpy as jnp
from jax import lax
from jax.experimental import pallas as pl
from jax.experimental.pallas import tpu as pltpu
from jax.sharding import Mesh
from jax.sharding import PartitionSpec as P

AXES = ("y", "x", "z", "core")
SIZES = (8, 4, 8, 2)
CH_AXES = ("z", "core")
PLANE = ("x", "z", "core")
MIB = 1024 * 1024
PARTS = 3


def spread_kernel(x_ref, v_ref, p_ref, limit_ref, out_ref):
    e = pl.program_id(0)
    both = jnp.concatenate([v_ref[0], p_ref[0]], axis=0).astype(jnp.float32)
    turned = both.T.astype(jnp.bfloat16)
    groups, _, per, lanes = out_ref.shape
    out_ref[...] = turned.reshape(groups, 1, per, lanes)

    @pl.when(e == pl.num_programs(0) - 1)
    def _():
        for k in range(groups):
            out_ref[k, 0] = limit_ref[...]


def spread(x_index, start, limits):
    energies, rows, width = start.shape
    cols = width // 8
    per = cols // 16
    return pl.pallas_call(
        spread_kernel,
        grid_spec=pltpu.PrefetchScalarGridSpec(
            num_scalar_prefetch=1,
            grid=(energies + 1,),
            in_specs=[
                pl.BlockSpec((1, rows, cols), lambda e, x: (jnp.minimum(e, energies - 1), 0, x[0])),
                pl.BlockSpec((1, rows, cols), lambda e, x: (jnp.minimum(e, energies - 1), 0, 4 + x[0])),
                pl.BlockSpec(limits.shape, lambda e, x: (0, 0)),
            ],
            out_specs=pl.BlockSpec((16, 1, per, 2 * rows), lambda e, x: (0, e, 0, 0)),
        ),
        out_shape=jax.ShapeDtypeStruct((16, energies + 1, per, 2 * rows), start.dtype),
        name="spread",
    )(x_index, start, start, limits)


def join_kernel(in_ref, out_ref):
    rows = out_ref.shape[1]
    low = lax.broadcasted_iota(jnp.int32, (rows, 128), 1) < 64
    for z in range(8):
        one = in_ref[2 * z, pl.ds(0, rows)].astype(jnp.float32)
        two = in_ref[2 * z + 1, pl.ds(0, rows)].astype(jnp.float32)
        lanes = pl.ds(128 * z, 128)
        out_ref[0, :, lanes] = jnp.where(low, one, pltpu.roll(two, 64, 1)).astype(out_ref.dtype)
        out_ref[1, :, lanes] = jnp.where(low, pltpu.roll(one, 64, 1), two).astype(out_ref.dtype)


def join(pieces, rows):
    return pl.pallas_call(
        join_kernel,
        out_shape=jax.ShapeDtypeStruct((2, rows, 1024), pieces.dtype),
        name="join",
    )(pieces)


def turn_kernel(*refs):
    out_ref = refs[-1]
    for q, ref in enumerate(refs[:-1]):
        groups, _, share, channels = ref.shape
        block = ref[...].reshape(groups * share, channels)
        out_ref[0, :, pl.ds(groups * share * q, groups * share)] = block.T


def turn(basis):
    groups, sectors, share, channels = basis.shape
    part = groups // 4
    specs = [pl.BlockSpec((part, 1, share, channels), lambda s, q=q: (q, s, 0, 0)) for q in range(4)]
    return pl.pallas_call(
        turn_kernel,
        grid=(sectors,),
        in_specs=specs,
        out_specs=pl.BlockSpec((1, channels, groups * share), lambda s: (s, 0, 0)),
        out_shape=jax.ShapeDtypeStruct((sectors, channels, groups * share), basis.dtype),
        compiler_params=pltpu.CompilerParams(vmem_limit_bytes=40 * MIB),
        name="turn",
    )(basis, basis, basis, basis)


def stage_kernel(pieces, parts, y_ref, state_ref, *refs):
    basis_refs, coef_ref = refs[:pieces], refs[pieces]
    next_refs, (out_ref, now, rot) = refs[-3 - parts : -3], refs[-3:]
    del y_ref
    s = pl.program_id(0)
    energies = coef_ref.shape[3]
    rows, channels = state_ref.shape[1:]
    own = rows // parts
    per = own // energies

    @pl.when(s == 0)
    def _():
        now[pl.ds(0, rows)] = state_ref[0]
        now[pl.ds(rows, rows)] = state_ref[1]

    for k in range(parts * energies):
        part, e = divmod(k, energies)
        cosine = coef_ref[part, 0, 0, pl.ds(e, 1), :]
        ratio = coef_ref[part, 0, 1, pl.ds(e, 1), :]
        product = coef_ref[part, 0, 2, pl.ds(e, 1), :]
        values = now[pl.ds(per * k, per), :].astype(jnp.float32)
        slopes = now[pl.ds(rows + per * k, per), :].astype(jnp.float32)
        rot[pl.ds(per * k, per), :] = (cosine * values + ratio * slopes).astype(rot.dtype)
        rot[pl.ds(rows + per * k, per), :] = (cosine * slopes - product * values).astype(rot.dtype)
    low = lax.broadcasted_iota(jnp.int32, (rows, 128), 1) < 64
    width = channels // pieces
    for q, basis_ref in enumerate(basis_refs):
        if pieces == 1:
            fresh = jnp.dot(rot[...], basis_ref[0], preferred_element_type=jnp.float32)
        else:
            block = basis_ref[...].reshape(width, channels)
            fresh = lax.dot_general(
                rot[...], block, (((1,), (1,)), ((), ())), preferred_element_type=jnp.float32
            )
        now[:, pl.ds(width * q, width)] = fresh.astype(now.dtype)
        for k in range(width // 128):
            z = width // 128 * q + k
            lanes = slice(128 * k, 128 * k + 128)
            values = fresh[:rows, lanes]
            slopes = fresh[rows:, lanes]
            one = jnp.where(low, values, pltpu.roll(slopes, 64, 1)).astype(out_ref.dtype)
            two = jnp.where(low, pltpu.roll(values, 64, 1), slopes).astype(out_ref.dtype)
            out_ref[0, 2 * z] = one.reshape(parts, own, 128)
            out_ref[0, 2 * z + 1] = two.reshape(parts, own, 128)

    @pl.when(s == pl.num_programs(0) - 1)
    def _():
        for part, next_ref in enumerate(next_refs):
            next_ref[0] = now[pl.ds(own * part, own)]
            next_ref[1] = now[pl.ds(rows + own * part, own)]


def stage(step, part, y_index, state, basis, coefs, kept):
    sectors = coefs.shape[1]
    _, rows, channels = state.shape
    first = step == 0
    pieces, parts = (4, PARTS) if first else (1, 1)
    own = rows // parts
    if first:
        groups, _, share, _ = basis.shape
        block = (groups // pieces, 1, share, channels)
        basis_specs = [pl.BlockSpec(block, lambda s, y, q=q: (q, s, 0, 0)) for q in range(pieces)]
    else:
        basis_specs = [pl.BlockSpec((1, channels, channels), lambda s, y: (s, 0, 0))]
    outs = pl.pallas_call(
        functools.partial(stage_kernel, pieces, parts),
        grid_spec=pltpu.PrefetchScalarGridSpec(
            num_scalar_prefetch=1,
            grid=(sectors,),
            in_specs=[pl.BlockSpec(state.shape, lambda s, y: (0, 0, 0))]
            + basis_specs
            + [pl.BlockSpec((parts, 1) + coefs.shape[2:], lambda s, y: (part, s, 0, 0, 0))]
            + ([] if first else [pl.BlockSpec(memory_space=pl.ANY)]),
            out_specs=[pl.BlockSpec((2, own, channels), lambda s, y: (0, 0, 0))] * parts
            + [
                pl.BlockSpec(
                    (1, 16, parts, own, 128),
                    lambda s, y: (jnp.where(y[0] == step, s, sectors), 0, part, 0, 0),
                ),
            ],
            scratch_shapes=[
                pltpu.VMEM((2 * rows, channels), state.dtype),
                pltpu.VMEM((2 * rows, channels), state.dtype),
            ],
        ),
        out_shape=[jax.ShapeDtypeStruct((2, own, channels), state.dtype)] * parts
        + [jax.ShapeDtypeStruct((sectors + 1, 16, PARTS, own, 128), state.dtype)],
        input_output_aliases={} if first else {4: 1},
        compiler_params=pltpu.CompilerParams(vmem_limit_bytes=(48 if first else 16) * MIB),
        name="stage",
    )(y_index, state, *[basis] * pieces, coefs, *([] if first else [kept]))
    return list(outs[:-1]), outs[-1]


def finish_kernel(in_ref, out_ref):
    groups, energies, per, lanes = in_ref.shape
    half = lanes // 2
    cols = groups * per
    for e in range(energies):
        turned = in_ref[:, e].reshape(cols, lanes).T
        out_ref[e, :, pl.ds(0, cols)] = turned[:half]
        out_ref[e, :, pl.ds(cols, cols)] = turned[half:]


def finish(pieces):
    groups, energies, per, lanes = pieces.shape
    batch = 2
    return pl.pallas_call(
        finish_kernel,
        grid=(energies // batch,),
        in_specs=[pl.BlockSpec((groups, batch, per, lanes), lambda e: (0, e, 0, 0))],
        out_specs=pl.BlockSpec((batch, lanes // 2, 2 * groups * per), lambda e: (e, 0, 0)),
        out_shape=jax.ShapeDtypeStruct((energies, lanes // 2, 2 * groups * per), pieces.dtype),
        compiler_params=pltpu.CompilerParams(vmem_limit_bytes=16 * MIB),
        name="finish",
    )(pieces)


def per_device(start_amps, energies, thresholds, intersection):
    planes = lax.axis_size("y")
    y_index = lax.axis_index("y").astype(jnp.int32).reshape(1)
    x_index = lax.axis_index("x").astype(jnp.int32).reshape(1)
    count = energies.shape[0]
    channels = intersection.shape[2]
    share = intersection.shape[1]
    extra = jnp.pad(thresholds, ((0, 7), (0, channels - share)))
    ring = lax.all_gather(jnp.concatenate([intersection[0], extra]), "x")
    basis = lax.all_gather(ring[:, :share], CH_AXES)
    limits = jnp.pad(ring[:, share, :share].reshape(2, 2 * share), ((0, 14), (0, 0)))

    blocks = spread(x_index, start_amps, limits)
    per, lanes = blocks.shape[2:]
    rows = count * per
    blocks = lax.all_to_all(blocks.reshape(16, rows + per, lanes), CH_AXES, 0, 0)
    state = join(blocks, rows)
    limits = blocks[:, rows : rows + 2].reshape(16, 4, share).swapaxes(0, 1).reshape(4, 1, channels)
    wave = jnp.sqrt(energies[None, :, None] - limits.astype(jnp.float32))
    sine = jnp.sin(wave)
    coefs = jnp.stack([jnp.cos(wave), sine / wave, wave * sine], axis=1)
    coefs = coefs.reshape(4, 3, PARTS, count // PARTS, channels).transpose(2, 0, 1, 3, 4)
    states, kept = stage(0, 0, y_index, state, basis, coefs, None)
    basis = turn(basis)
    for step in range(1, planes):
        for part in range(PARTS):
            state = lax.ppermute(states[part], "y", [(step - 1, step)])
            (states[part],), kept = stage(step, part, y_index, state, basis, coefs, kept)
    back = lax.all_to_all(kept[:4].reshape(64, rows, lanes), PLANE, 0, 0)
    return finish(back.reshape(64, count, per, lanes))[None]


def solution(mesh):
    fine = Mesh(mesh.devices.reshape(SIZES), AXES)
    sec, ch = ("y", "x"), CH_AXES
    in_specs = (P(None, ch, None), P(), P(sec, ch), P(sec, ch, None))
    out_specs = P(sec, None, ch, None)
    return jax.shard_map(
        per_device, mesh=fine, in_specs=in_specs, out_specs=out_specs, check_vma=False
    )
```

```python
import functools

import jax
import jax.numpy as jnp
from jax import lax
from jax.experimental import pallas as pl
from jax.experimental.pallas import tpu as pltpu
from jax.sharding import Mesh
from jax.sharding import PartitionSpec as P

AXES = ("y", "x", "z", "core")
SIZES = (8, 4, 8, 2)
CH_AXES = ("z", "core")
PLANE = ("x", "z", "core")
MIB = 1024 * 1024
PARTS = 3


def spread_kernel(x_ref, v_ref, p_ref, limit_ref, out_ref):
    e = pl.program_id(0)
    both = jnp.concatenate([v_ref[0], p_ref[0]], axis=0).astype(jnp.float32)
    turned = both.T.astype(jnp.bfloat16)
    groups, _, per, lanes = out_ref.shape
    out_ref[...] = turned.reshape(groups, 1, per, lanes)

    @pl.when(e == pl.num_programs(0) - 1)
    def _():
        for k in range(groups):
            out_ref[k, 0] = limit_ref[...]


def spread(x_index, start, limits):
    energies, rows, width = start.shape
    cols = width // 8
    per = cols // 16
    return pl.pallas_call(
        spread_kernel,
        grid_spec=pltpu.PrefetchScalarGridSpec(
            num_scalar_prefetch=1,
            grid=(energies + 1,),
            in_specs=[
                pl.BlockSpec((1, rows, cols), lambda e, x: (jnp.minimum(e, energies - 1), 0, x[0])),
                pl.BlockSpec((1, rows, cols), lambda e, x: (jnp.minimum(e, energies - 1), 0, 4 + x[0])),
                pl.BlockSpec(limits.shape, lambda e, x: (0, 0)),
            ],
            out_specs=pl.BlockSpec((16, 1, per, 2 * rows), lambda e, x: (0, e, 0, 0)),
        ),
        out_shape=jax.ShapeDtypeStruct((16, energies + 1, per, 2 * rows), start.dtype),
        name="spread",
    )(x_index, start, start, limits)


def join_kernel(in_ref, out_ref):
    rows = out_ref.shape[1]
    low = lax.broadcasted_iota(jnp.int32, (rows, 128), 1) < 64
    for z in range(8):
        one = in_ref[2 * z, pl.ds(0, rows)].astype(jnp.float32)
        two = in_ref[2 * z + 1, pl.ds(0, rows)].astype(jnp.float32)
        lanes = pl.ds(128 * z, 128)
        out_ref[0, :, lanes] = jnp.where(low, one, pltpu.roll(two, 64, 1)).astype(out_ref.dtype)
        out_ref[1, :, lanes] = jnp.where(low, pltpu.roll(one, 64, 1), two).astype(out_ref.dtype)


def join(pieces, rows):
    return pl.pallas_call(
        join_kernel,
        out_shape=jax.ShapeDtypeStruct((2, rows, 1024), pieces.dtype),
        name="join",
    )(pieces)


def turn_kernel(*refs):
    out_ref = refs[-1]
    for q, ref in enumerate(refs[:-1]):
        groups, _, share, channels = ref.shape
        block = ref[...].reshape(groups * share, channels)
        out_ref[0, :, pl.ds(groups * share * q, groups * share)] = block.T


def turn(basis):
    groups, sectors, share, channels = basis.shape
    part = groups // 4
    specs = [pl.BlockSpec((part, 1, share, channels), lambda s, q=q: (q, s, 0, 0)) for q in range(4)]
    return pl.pallas_call(
        turn_kernel,
        grid=(sectors,),
        in_specs=specs,
        out_specs=pl.BlockSpec((1, channels, groups * share), lambda s: (s, 0, 0)),
        out_shape=jax.ShapeDtypeStruct((sectors, channels, groups * share), basis.dtype),
        compiler_params=pltpu.CompilerParams(vmem_limit_bytes=40 * MIB),
        name="turn",
    )(basis, basis, basis, basis)


def stage_kernel(step, pieces, parts, y_ref, state_ref, *refs):
    basis_refs, coef_ref = refs[:pieces], refs[pieces]
    next_refs, (out_ref, now, rot) = refs[-3 - parts : -3], refs[-3:]
    s = pl.program_id(0)
    energies = coef_ref.shape[3]
    rows, channels = state_ref.shape[1:]
    own = rows // parts
    per = own // energies

    @pl.when(y_ref[0] == step)
    def _():
        @pl.when(s == 0)
        def _():
            now[pl.ds(0, rows)] = state_ref[0]
            now[pl.ds(rows, rows)] = state_ref[1]

        for k in range(parts * energies):
            part, e = divmod(k, energies)
            cosine = coef_ref[part, 0, 0, pl.ds(e, 1), :]
            ratio = coef_ref[part, 0, 1, pl.ds(e, 1), :]
            product = coef_ref[part, 0, 2, pl.ds(e, 1), :]
            values = now[pl.ds(per * k, per), :].astype(jnp.float32)
            slopes = now[pl.ds(rows + per * k, per), :].astype(jnp.float32)
            rot[pl.ds(per * k, per), :] = (cosine * values + ratio * slopes).astype(rot.dtype)
            rot[pl.ds(rows + per * k, per), :] = (cosine * slopes - product * values).astype(rot.dtype)
        low = lax.broadcasted_iota(jnp.int32, (rows, 128), 1) < 64
        width = channels // pieces
        for q, basis_ref in enumerate(basis_refs):
            if pieces == 1:
                fresh = jnp.dot(rot[...], basis_ref[0], preferred_element_type=jnp.float32)
            else:
                block = basis_ref[...].reshape(width, channels)
                fresh = lax.dot_general(
                    rot[...], block, (((1,), (1,)), ((), ())), preferred_element_type=jnp.float32
                )
            now[:, pl.ds(width * q, width)] = fresh.astype(now.dtype)
            for k in range(width // 128):
                z = width // 128 * q + k
                lanes = slice(128 * k, 128 * k + 128)
                values = fresh[:rows, lanes]
                slopes = fresh[rows:, lanes]
                one = jnp.where(low, values, pltpu.roll(slopes, 64, 1)).astype(out_ref.dtype)
                two = jnp.where(low, pltpu.roll(values, 64, 1), slopes).astype(out_ref.dtype)
                out_ref[0, 2 * z] = one.reshape(parts, own, 128)
                out_ref[0, 2 * z + 1] = two.reshape(parts, own, 128)

        @pl.when(s == pl.num_programs(0) - 1)
        def _():
            for part, next_ref in enumerate(next_refs):
                next_ref[0] = now[pl.ds(own * part, own)]
                next_ref[1] = now[pl.ds(rows + own * part, own)]


def stage(step, part, y_index, state, basis, coefs, kept):
    sectors = coefs.shape[1]
    _, rows, channels = state.shape
    first = step == 0
    pieces, parts = (4, PARTS) if first else (1, 1)
    own = rows // parts
    if first:
        groups, _, share, _ = basis.shape
        block = (groups // pieces, 1, share, channels)
        basis_specs = [pl.BlockSpec(block, lambda s, y, q=q: (q, s, 0, 0)) for q in range(pieces)]
    else:
        basis_specs = [
            pl.BlockSpec(
                (1, channels, channels), lambda s, y: (jnp.where(y[0] == step, s, 0), 0, 0)
            )
        ]
    outs = pl.pallas_call(
        functools.partial(stage_kernel, step, pieces, parts),
        grid_spec=pltpu.PrefetchScalarGridSpec(
            num_scalar_prefetch=1,
            grid=(sectors,),
            in_specs=[pl.BlockSpec(state.shape, lambda s, y: (0, 0, 0))]
            + basis_specs
            + [pl.BlockSpec((parts, 1) + coefs.shape[2:], lambda s, y: (part, s, 0, 0, 0))]
            + ([] if first else [pl.BlockSpec(memory_space=pl.ANY)]),
            out_specs=[pl.BlockSpec((2, own, channels), lambda s, y: (0, 0, 0))] * parts
            + [
                pl.BlockSpec(
                    (1, 16, parts, own, 128),
                    lambda s, y: (jnp.where(y[0] == step, s, sectors), 0, part, 0, 0),
                ),
            ],
            scratch_shapes=[
                pltpu.VMEM((2 * rows, channels), state.dtype),
                pltpu.VMEM((2 * rows, channels), state.dtype),
            ],
        ),
        out_shape=[jax.ShapeDtypeStruct((2, own, channels), state.dtype)] * parts
        + [jax.ShapeDtypeStruct((sectors + 1, 16, PARTS, own, 128), state.dtype)],
        input_output_aliases={} if first else {4: 1},
        compiler_params=pltpu.CompilerParams(vmem_limit_bytes=(48 if first else 16) * MIB),
        name="stage",
    )(y_index, state, *[basis] * pieces, coefs, *([] if first else [kept]))
    return list(outs[:-1]), outs[-1]


def finish_kernel(in_ref, out_ref):
    groups, energies, per, lanes = in_ref.shape
    half = lanes // 2
    cols = groups * per
    for e in range(energies):
        turned = in_ref[:, e].reshape(cols, lanes).T
        out_ref[e, :, pl.ds(0, cols)] = turned[:half]
        out_ref[e, :, pl.ds(cols, cols)] = turned[half:]


def finish(pieces):
    groups, energies, per, lanes = pieces.shape
    batch = 2
    return pl.pallas_call(
        finish_kernel,
        grid=(energies // batch,),
        in_specs=[pl.BlockSpec((groups, batch, per, lanes), lambda e: (0, e, 0, 0))],
        out_specs=pl.BlockSpec((batch, lanes // 2, 2 * groups * per), lambda e: (e, 0, 0)),
        out_shape=jax.ShapeDtypeStruct((energies, lanes // 2, 2 * groups * per), pieces.dtype),
        compiler_params=pltpu.CompilerParams(vmem_limit_bytes=16 * MIB),
        name="finish",
    )(pieces)


def per_device(start_amps, energies, thresholds, intersection):
    planes = lax.axis_size("y")
    y_index = lax.axis_index("y").astype(jnp.int32).reshape(1)
    x_index = lax.axis_index("x").astype(jnp.int32).reshape(1)
    count = energies.shape[0]
    channels = intersection.shape[2]
    share = intersection.shape[1]
    extra = jnp.pad(thresholds, ((0, 7), (0, channels - share)))
    ring = lax.all_gather(jnp.concatenate([intersection[0], extra]), "x")
    basis = lax.all_gather(ring[:, :share], CH_AXES)
    limits = jnp.pad(ring[:, share, :share].reshape(2, 2 * share), ((0, 14), (0, 0)))

    blocks = spread(x_index, start_amps, limits)
    per, lanes = blocks.shape[2:]
    rows = count * per
    blocks = lax.all_to_all(blocks.reshape(16, rows + per, lanes), CH_AXES, 0, 0)
    state = join(blocks, rows)
    limits = blocks[:, rows : rows + 2].reshape(16, 4, share).swapaxes(0, 1).reshape(4, 1, channels)
    wave = jnp.sqrt(energies[None, :, None] - limits.astype(jnp.float32))
    sine = jnp.sin(wave)
    coefs = jnp.stack([jnp.cos(wave), sine / wave, wave * sine], axis=1)
    coefs = coefs.reshape(4, 3, PARTS, count // PARTS, channels).transpose(2, 0, 1, 3, 4)
    states, kept = stage(0, 0, y_index, state, basis, coefs, None)
    basis = turn(basis)
    for step in range(1, planes):
        for part in range(PARTS):
            state = lax.ppermute(states[part], "y", [(step - 1, step)])
            (states[part],), kept = stage(step, part, y_index, state, basis, coefs, kept)
    back = lax.all_to_all(kept[:4].reshape(64, rows, lanes), PLANE, 0, 0)
    return finish(back.reshape(64, count, per, lanes))[None]


def solution(mesh):
    fine = Mesh(mesh.devices.reshape(SIZES), AXES)
    sec, ch = ("y", "x"), CH_AXES
    in_specs = (P(None, ch, None), P(), P(sec, ch), P(sec, ch, None))
    out_specs = P(sec, None, ch, None)
    return jax.shard_map(
        per_device, mesh=fine, in_specs=in_specs, out_specs=out_specs, check_vma=False
    )
```

```python
import functools

import jax
import jax.numpy as jnp
from jax import lax
from jax.experimental import pallas as pl
from jax.experimental.pallas import tpu as pltpu
from jax.sharding import Mesh
from jax.sharding import PartitionSpec as P

AXES = ("y", "x", "z", "core")
SIZES = (8, 4, 8, 2)
CH_AXES = ("z", "core")
PLANE = ("x", "z", "core")
MIB = 1024 * 1024
PARTS = 3


def spread_kernel(x_ref, v_ref, p_ref, limit_ref, out_ref):
    e = pl.program_id(0)
    both = jnp.concatenate([v_ref[0], p_ref[0]], axis=0).astype(jnp.float32)
    turned = both.T.astype(jnp.bfloat16)
    groups, _, per, lanes = out_ref.shape
    out_ref[...] = turned.reshape(groups, 1, per, lanes)

    @pl.when(e == pl.num_programs(0) - 1)
    def _():
        for k in range(groups):
            out_ref[k, 0] = limit_ref[...]


def spread(x_index, start, limits):
    energies, rows, width = start.shape
    cols = width // 8
    per = cols // 16
    return pl.pallas_call(
        spread_kernel,
        grid_spec=pltpu.PrefetchScalarGridSpec(
            num_scalar_prefetch=1,
            grid=(energies + 1,),
            in_specs=[
                pl.BlockSpec((1, rows, cols), lambda e, x: (jnp.minimum(e, energies - 1), 0, x[0])),
                pl.BlockSpec((1, rows, cols), lambda e, x: (jnp.minimum(e, energies - 1), 0, 4 + x[0])),
                pl.BlockSpec(limits.shape, lambda e, x: (0, 0)),
            ],
            out_specs=pl.BlockSpec((16, 1, per, 2 * rows), lambda e, x: (0, e, 0, 0)),
        ),
        out_shape=jax.ShapeDtypeStruct((16, energies + 1, per, 2 * rows), start.dtype),
        name="spread",
    )(x_index, start, start, limits)


def join_kernel(in_ref, out_ref):
    rows = out_ref.shape[1]
    low = lax.broadcasted_iota(jnp.int32, (rows, 128), 1) < 64
    for z in range(8):
        one = in_ref[2 * z, pl.ds(0, rows)].astype(jnp.float32)
        two = in_ref[2 * z + 1, pl.ds(0, rows)].astype(jnp.float32)
        lanes = pl.ds(128 * z, 128)
        out_ref[0, :, lanes] = jnp.where(low, one, pltpu.roll(two, 64, 1)).astype(out_ref.dtype)
        out_ref[1, :, lanes] = jnp.where(low, pltpu.roll(one, 64, 1), two).astype(out_ref.dtype)


def join(pieces, rows):
    return pl.pallas_call(
        join_kernel,
        out_shape=jax.ShapeDtypeStruct((2, rows, 1024), pieces.dtype),
        compiler_params=pltpu.CompilerParams(vmem_limit_bytes=8 * MIB),
        name="join",
    )(pieces)


def turn_kernel(*refs):
    out_ref = refs[-1]
    for q, ref in enumerate(refs[:-1]):
        groups, _, share, channels = ref.shape
        block = ref[...].reshape(groups * share, channels)
        out_ref[0, :, pl.ds(groups * share * q, groups * share)] = block.T


def turn(basis):
    groups, sectors, share, channels = basis.shape
    part = groups // 4
    specs = [pl.BlockSpec((part, 1, share, channels), lambda s, q=q: (q, s, 0, 0)) for q in range(4)]
    return pl.pallas_call(
        turn_kernel,
        grid=(sectors,),
        in_specs=specs,
        out_specs=pl.BlockSpec((1, channels, groups * share), lambda s: (s, 0, 0)),
        out_shape=jax.ShapeDtypeStruct((sectors, channels, groups * share), basis.dtype),
        compiler_params=pltpu.CompilerParams(vmem_limit_bytes=40 * MIB),
        name="turn",
    )(basis, basis, basis, basis)


def stage_kernel(step, pieces, parts, handed, y_ref, state_ref, *refs):
    basis_refs, coef_ref = refs[:pieces], refs[pieces]
    next_refs, (out_ref, now, rot) = refs[-3 - handed : -3], refs[-3:]
    s = pl.program_id(0)
    energies = coef_ref.shape[3]
    rows, channels = state_ref.shape[1:]
    own = rows // parts
    per = own // energies

    @pl.when(y_ref[0] == step)
    def _():
        @pl.when(s == 0)
        def _():
            now[pl.ds(0, rows)] = state_ref[0]
            now[pl.ds(rows, rows)] = state_ref[1]

        for k in range(parts * energies):
            part, e = divmod(k, energies)
            cosine = coef_ref[part, 0, 0, pl.ds(e, 1), :]
            ratio = coef_ref[part, 0, 1, pl.ds(e, 1), :]
            product = coef_ref[part, 0, 2, pl.ds(e, 1), :]
            values = now[pl.ds(per * k, per), :].astype(jnp.float32)
            slopes = now[pl.ds(rows + per * k, per), :].astype(jnp.float32)
            rot[pl.ds(per * k, per), :] = (cosine * values + ratio * slopes).astype(rot.dtype)
            rot[pl.ds(rows + per * k, per), :] = (cosine * slopes - product * values).astype(rot.dtype)
        low = lax.broadcasted_iota(jnp.int32, (rows, 128), 1) < 64
        width = channels // pieces
        for q, basis_ref in enumerate(basis_refs):
            if pieces == 1:
                fresh = jnp.dot(rot[...], basis_ref[0], preferred_element_type=jnp.float32)
            else:
                block = basis_ref[...].reshape(width, channels)
                fresh = lax.dot_general(
                    rot[...], block, (((1,), (1,)), ((), ())), preferred_element_type=jnp.float32
                )
            now[:, pl.ds(width * q, width)] = fresh.astype(now.dtype)
            for k in range(width // 128):
                z = width // 128 * q + k
                lanes = slice(128 * k, 128 * k + 128)
                values = fresh[:rows, lanes]
                slopes = fresh[rows:, lanes]
                one = jnp.where(low, values, pltpu.roll(slopes, 64, 1)).astype(out_ref.dtype)
                two = jnp.where(low, pltpu.roll(values, 64, 1), slopes).astype(out_ref.dtype)
                out_ref[0, 2 * z] = one.reshape(parts, own, 128)
                out_ref[0, 2 * z + 1] = two.reshape(parts, own, 128)

        @pl.when(s == pl.num_programs(0) - 1)
        def _():
            for part, next_ref in enumerate(next_refs):
                next_ref[0] = now[pl.ds(own * part, own)]
                next_ref[1] = now[pl.ds(rows + own * part, own)]


def stage(step, part, last, y_index, state, basis, coefs, kept):
    sectors = coefs.shape[1]
    _, rows, channels = state.shape
    first = step == 0
    pieces, parts = (4, PARTS) if first else (1, 1)
    own = rows // parts
    handed = 0 if last else parts
    if first:
        groups, _, share, _ = basis.shape
        block = (groups // pieces, 1, share, channels)
        basis_specs = [pl.BlockSpec(block, lambda s, y, q=q: (q, s, 0, 0)) for q in range(pieces)]
    else:
        basis_specs = [
            pl.BlockSpec(
                (1, channels, channels), lambda s, y: (jnp.where(y[0] == step, s, 0), 0, 0)
            )
        ]
    outs = pl.pallas_call(
        functools.partial(stage_kernel, step, pieces, parts, handed),
        grid_spec=pltpu.PrefetchScalarGridSpec(
            num_scalar_prefetch=1,
            grid=(sectors,),
            in_specs=[pl.BlockSpec(state.shape, lambda s, y: (0, 0, 0))]
            + basis_specs
            + [pl.BlockSpec((parts, 1) + coefs.shape[2:], lambda s, y: (part, s, 0, 0, 0))]
            + ([] if first else [pl.BlockSpec(memory_space=pl.ANY)]),
            out_specs=[pl.BlockSpec((2, own, channels), lambda s, y: (0, 0, 0))] * handed
            + [
                pl.BlockSpec(
                    (1, 16, parts, own, 128),
                    lambda s, y: (jnp.where(y[0] == step, s, sectors), 0, part, 0, 0),
                ),
            ],
            scratch_shapes=[
                pltpu.VMEM((2 * rows, channels), state.dtype),
                pltpu.VMEM((2 * rows, channels), state.dtype),
            ],
        ),
        out_shape=[jax.ShapeDtypeStruct((2, own, channels), state.dtype)] * handed
        + [jax.ShapeDtypeStruct((sectors + 1, 16, PARTS, own, 128), state.dtype)],
        input_output_aliases={} if first else {4: handed},
        compiler_params=pltpu.CompilerParams(vmem_limit_bytes=(48 if first else 16) * MIB),
        name="stage",
    )(y_index, state, *[basis] * pieces, coefs, *([] if first else [kept]))
    return list(outs[:-1]), outs[-1]


def finish_kernel(in_ref, out_ref):
    groups, energies, per, lanes = in_ref.shape
    half = lanes // 2
    cols = groups * per
    for e in range(energies):
        turned = in_ref[:, e].reshape(cols, lanes).T
        out_ref[e, :, pl.ds(0, cols)] = turned[:half]
        out_ref[e, :, pl.ds(cols, cols)] = turned[half:]


def finish(pieces):
    groups, energies, per, lanes = pieces.shape
    batch = 2
    return pl.pallas_call(
        finish_kernel,
        grid=(energies // batch,),
        in_specs=[pl.BlockSpec((groups, batch, per, lanes), lambda e: (0, e, 0, 0))],
        out_specs=pl.BlockSpec((batch, lanes // 2, 2 * groups * per), lambda e: (e, 0, 0)),
        out_shape=jax.ShapeDtypeStruct((energies, lanes // 2, 2 * groups * per), pieces.dtype),
        compiler_params=pltpu.CompilerParams(vmem_limit_bytes=16 * MIB),
        name="finish",
    )(pieces)


def around_x(values):
    size = lax.axis_size("x")
    moved = [values] + [
        lax.ppermute(values, "x", [(k, (k + shift) % size) for k in range(size)])
        for shift in range(size - 1, 0, -1)
    ]
    start = lax.rem(size - lax.axis_index("x"), size)
    return lax.dynamic_slice_in_dim(jnp.concatenate(moved + moved), start, size)


def per_device(start_amps, energies, thresholds, intersection):
    planes = lax.axis_size("y")
    y_index = lax.axis_index("y").astype(jnp.int32).reshape(1)
    x_index = lax.axis_index("x").astype(jnp.int32).reshape(1)
    count = energies.shape[0]
    channels = intersection.shape[2]
    share = intersection.shape[1]
    ring = lax.all_gather(intersection[0], "x")
    basis = lax.all_gather(ring, CH_AXES)
    limits = around_x(lax.optimization_barrier((thresholds, ring))[0])
    limits = jnp.pad(limits.reshape(2, 2 * share), ((0, 14), (0, 0)))

    blocks = spread(x_index, start_amps, limits)
    per, lanes = blocks.shape[2:]
    rows = count * per
    blocks = lax.all_to_all(blocks.reshape(16, rows + per, lanes), CH_AXES, 0, 0)
    limits = blocks[:, rows : rows + 2].reshape(16, 4, share).swapaxes(0, 1).reshape(4, 1, channels)
    wave = jnp.sqrt(energies[None, :, None] - limits.astype(jnp.float32))
    sine = jnp.sin(wave)
    coefs = jnp.stack([jnp.cos(wave), sine / wave, wave * sine], axis=1)
    coefs = coefs.reshape(4, 3, PARTS, count // PARTS, channels).transpose(2, 0, 1, 3, 4)
    blocks, coefs = lax.optimization_barrier((blocks, coefs))
    state = join(blocks, rows)
    states, kept = stage(0, 0, False, y_index, state, basis, coefs, None)
    basis = turn(basis)
    for step in range(1, planes):
        last = step == planes - 1
        for part in range(PARTS):
            state = lax.ppermute(states[part], "y", [(step - 1, step)])
            fresh, kept = stage(step, part, last, y_index, state, basis, coefs, kept)
            states[part] = None if last else fresh[0]
    back = lax.all_to_all(kept[:4].reshape(64, rows, lanes), PLANE, 0, 0)
    return finish(back.reshape(64, count, per, lanes))[None]


def solution(mesh):
    fine = Mesh(mesh.devices.reshape(SIZES), AXES)
    sec, ch = ("y", "x"), CH_AXES
    in_specs = (P(None, ch, None), P(), P(sec, ch), P(sec, ch, None))
    out_specs = P(sec, None, ch, None)
    return jax.shard_map(
        per_device, mesh=fine, in_specs=in_specs, out_specs=out_specs, check_vma=False
    )
```

```python
import functools

import jax
import jax.numpy as jnp
from jax import lax
from jax.experimental import pallas as pl
from jax.experimental.pallas import tpu as pltpu
from jax.sharding import Mesh
from jax.sharding import PartitionSpec as P

AXES = ("y", "x", "z", "core")
SIZES = (8, 4, 8, 2)
CH_AXES = ("z", "core")
PLANE = ("x", "z", "core")
MIB = 1024 * 1024
PARTS = 3


def spread_kernel(x_ref, v_ref, p_ref, limit_ref, out_ref):
    e = pl.program_id(0)
    both = jnp.concatenate([v_ref[0], p_ref[0]], axis=0).astype(jnp.float32)
    turned = both.T.astype(jnp.bfloat16)
    groups, _, per, lanes = out_ref.shape
    out_ref[...] = turned.reshape(groups, 1, per, lanes)

    @pl.when(e == pl.num_programs(0) - 1)
    def _():
        for k in range(groups):
            out_ref[k, 0] = limit_ref[...]


def spread(x_index, start, limits):
    energies, rows, width = start.shape
    cols = width // 8
    per = cols // 16
    return pl.pallas_call(
        spread_kernel,
        grid_spec=pltpu.PrefetchScalarGridSpec(
            num_scalar_prefetch=1,
            grid=(energies + 1,),
            in_specs=[
                pl.BlockSpec((1, rows, cols), lambda e, x: (jnp.minimum(e, energies - 1), 0, x[0])),
                pl.BlockSpec((1, rows, cols), lambda e, x: (jnp.minimum(e, energies - 1), 0, 4 + x[0])),
                pl.BlockSpec(limits.shape, lambda e, x: (0, 0)),
            ],
            out_specs=pl.BlockSpec((16, 1, per, 2 * rows), lambda e, x: (0, e, 0, 0)),
        ),
        out_shape=jax.ShapeDtypeStruct((16, energies + 1, per, 2 * rows), start.dtype),
        name="spread",
    )(x_index, start, start, limits)


def join_kernel(in_ref, out_ref):
    rows = out_ref.shape[1]
    low = lax.broadcasted_iota(jnp.int32, (rows, 128), 1) < 64
    for z in range(8):
        one = in_ref[2 * z, pl.ds(0, rows)].astype(jnp.float32)
        two = in_ref[2 * z + 1, pl.ds(0, rows)].astype(jnp.float32)
        lanes = pl.ds(128 * z, 128)
        out_ref[0, :, lanes] = jnp.where(low, one, pltpu.roll(two, 64, 1)).astype(out_ref.dtype)
        out_ref[1, :, lanes] = jnp.where(low, pltpu.roll(one, 64, 1), two).astype(out_ref.dtype)


def join(pieces, rows):
    return pl.pallas_call(
        join_kernel,
        out_shape=jax.ShapeDtypeStruct((2, rows, 1024), pieces.dtype),
        compiler_params=pltpu.CompilerParams(vmem_limit_bytes=8 * MIB),
        name="join",
    )(pieces)


def turn_kernel(*refs):
    out_ref = refs[-1]
    for q, ref in enumerate(refs[:-1]):
        groups, _, share, channels = ref.shape
        block = ref[...].reshape(groups * share, channels)
        out_ref[0, :, pl.ds(groups * share * q, groups * share)] = block.T


def turn(basis):
    groups, sectors, share, channels = basis.shape
    part = groups // 4
    specs = [pl.BlockSpec((part, 1, share, channels), lambda s, q=q: (q, s, 0, 0)) for q in range(4)]
    return pl.pallas_call(
        turn_kernel,
        grid=(sectors,),
        in_specs=specs,
        out_specs=pl.BlockSpec((1, channels, groups * share), lambda s: (s, 0, 0)),
        out_shape=jax.ShapeDtypeStruct((sectors, channels, groups * share), basis.dtype),
        compiler_params=pltpu.CompilerParams(vmem_limit_bytes=40 * MIB),
        cost_estimate=pl.CostEstimate(flops=0, bytes_accessed=2 * basis.size, transcendentals=0),
        name="turn",
    )(basis, basis, basis, basis)


def stage_kernel(step, pieces, parts, handed, y_ref, state_ref, *refs):
    basis_refs, coef_ref = refs[:pieces], refs[pieces]
    next_refs, (out_ref, now, rot) = refs[-3 - handed : -3], refs[-3:]
    s = pl.program_id(0)
    energies = coef_ref.shape[3]
    rows, channels = state_ref.shape[1:]
    own = rows // parts
    per = own // energies

    @pl.when(y_ref[0] == step)
    def _():
        @pl.when(s == 0)
        def _():
            now[pl.ds(0, rows)] = state_ref[0]
            now[pl.ds(rows, rows)] = state_ref[1]

        for k in range(parts * energies):
            part, e = divmod(k, energies)
            cosine = coef_ref[part, 0, 0, pl.ds(e, 1), :]
            ratio = coef_ref[part, 0, 1, pl.ds(e, 1), :]
            product = coef_ref[part, 0, 2, pl.ds(e, 1), :]
            values = now[pl.ds(per * k, per), :].astype(jnp.float32)
            slopes = now[pl.ds(rows + per * k, per), :].astype(jnp.float32)
            rot[pl.ds(per * k, per), :] = (cosine * values + ratio * slopes).astype(rot.dtype)
            rot[pl.ds(rows + per * k, per), :] = (cosine * slopes - product * values).astype(rot.dtype)
        low = lax.broadcasted_iota(jnp.int32, (rows, 128), 1) < 64
        width = channels // pieces
        for q, basis_ref in enumerate(basis_refs):
            if pieces == 1:
                fresh = jnp.dot(rot[...], basis_ref[0], preferred_element_type=jnp.float32)
            else:
                block = basis_ref[...].reshape(width, channels)
                fresh = lax.dot_general(
                    rot[...], block, (((1,), (1,)), ((), ())), preferred_element_type=jnp.float32
                )
            now[:, pl.ds(width * q, width)] = fresh.astype(now.dtype)
            for k in range(width // 128):
                z = width // 128 * q + k
                lanes = slice(128 * k, 128 * k + 128)
                values = fresh[:rows, lanes]
                slopes = fresh[rows:, lanes]
                one = jnp.where(low, values, pltpu.roll(slopes, 64, 1)).astype(out_ref.dtype)
                two = jnp.where(low, pltpu.roll(values, 64, 1), slopes).astype(out_ref.dtype)
                out_ref[0, 2 * z] = one.reshape(parts, own, 128)
                out_ref[0, 2 * z + 1] = two.reshape(parts, own, 128)

        @pl.when(s == pl.num_programs(0) - 1)
        def _():
            for part, next_ref in enumerate(next_refs):
                next_ref[0] = now[pl.ds(own * part, own)]
                next_ref[1] = now[pl.ds(rows + own * part, own)]


def stage(step, part, last, y_index, state, basis, coefs, kept):
    sectors = coefs.shape[1]
    _, rows, channels = state.shape
    first = step == 0
    pieces, parts = (4, PARTS) if first else (1, 1)
    own = rows // parts
    handed = 0 if last else parts
    if first:
        groups, _, share, _ = basis.shape
        block = (groups // pieces, 1, share, channels)
        basis_specs = [pl.BlockSpec(block, lambda s, y, q=q: (q, s, 0, 0)) for q in range(pieces)]
    else:
        basis_specs = [
            pl.BlockSpec(
                (1, channels, channels), lambda s, y: (jnp.where(y[0] == step, s, 0), 0, 0)
            )
        ]
    outs = pl.pallas_call(
        functools.partial(stage_kernel, step, pieces, parts, handed),
        grid_spec=pltpu.PrefetchScalarGridSpec(
            num_scalar_prefetch=1,
            grid=(sectors,),
            in_specs=[pl.BlockSpec(state.shape, lambda s, y: (0, 0, 0))]
            + basis_specs
            + [pl.BlockSpec((parts, 1) + coefs.shape[2:], lambda s, y: (part, s, 0, 0, 0))]
            + ([] if first else [pl.BlockSpec(memory_space=pl.ANY)]),
            out_specs=[pl.BlockSpec((2, own, channels), lambda s, y: (0, 0, 0))] * handed
            + [
                pl.BlockSpec(
                    (1, 16, parts, own, 128),
                    lambda s, y: (jnp.where(y[0] == step, s, sectors), 0, part, 0, 0),
                ),
            ],
            scratch_shapes=[
                pltpu.VMEM((2 * rows, channels), state.dtype),
                pltpu.VMEM((2 * rows, channels), state.dtype),
            ],
        ),
        out_shape=[jax.ShapeDtypeStruct((2, own, channels), state.dtype)] * handed
        + [jax.ShapeDtypeStruct((sectors + 1, 16, PARTS, own, 128), state.dtype)],
        input_output_aliases={} if first else {4: handed},
        compiler_params=pltpu.CompilerParams(vmem_limit_bytes=(48 if first else 16) * MIB),
        cost_estimate=pl.CostEstimate(
            flops=4 * sectors * rows * channels * channels,
            bytes_accessed=2 * sectors * channels * (channels + 2 * rows),
            transcendentals=0,
        ),
        name="stage",
    )(y_index, state, *[basis] * pieces, coefs, *([] if first else [kept]))
    return list(outs[:-1]), outs[-1]


def finish_kernel(in_ref, out_ref):
    groups, energies, per, lanes = in_ref.shape
    half = lanes // 2
    cols = groups * per
    for e in range(energies):
        turned = in_ref[:, e].reshape(cols, lanes).T
        out_ref[e, :, pl.ds(0, cols)] = turned[:half]
        out_ref[e, :, pl.ds(cols, cols)] = turned[half:]


def finish(pieces):
    groups, energies, per, lanes = pieces.shape
    batch = 2
    return pl.pallas_call(
        finish_kernel,
        grid=(energies // batch,),
        in_specs=[pl.BlockSpec((groups, batch, per, lanes), lambda e: (0, e, 0, 0))],
        out_specs=pl.BlockSpec((batch, lanes // 2, 2 * groups * per), lambda e: (e, 0, 0)),
        out_shape=jax.ShapeDtypeStruct((energies, lanes // 2, 2 * groups * per), pieces.dtype),
        compiler_params=pltpu.CompilerParams(vmem_limit_bytes=16 * MIB),
        name="finish",
    )(pieces)


def per_device(start_amps, energies, thresholds, intersection):
    planes = lax.axis_size("y")
    y_index = lax.axis_index("y").astype(jnp.int32).reshape(1)
    x_index = lax.axis_index("x").astype(jnp.int32).reshape(1)
    count = energies.shape[0]
    channels = intersection.shape[2]
    share = intersection.shape[1]
    extra = jnp.pad(thresholds, ((0, 7), (0, channels - share)))
    ring = lax.all_gather(jnp.concatenate([intersection[0], extra]), "x")
    basis = lax.all_gather(ring[:, :share], CH_AXES)
    limits = jnp.pad(ring[:, share, :share].reshape(2, 2 * share), ((0, 14), (0, 0)))

    blocks = spread(x_index, start_amps, limits)
    per, lanes = blocks.shape[2:]
    rows = count * per
    blocks = lax.all_to_all(blocks.reshape(16, rows + per, lanes), CH_AXES, 0, 0)
    limits = blocks[:, rows : rows + 2].reshape(16, 4, share).swapaxes(0, 1).reshape(4, 1, channels)
    wave = jnp.sqrt(energies[None, :, None] - limits.astype(jnp.float32))
    sine = jnp.sin(wave)
    coefs = jnp.stack([jnp.cos(wave), sine / wave, wave * sine], axis=1)
    coefs = coefs.reshape(4, 3, PARTS, count // PARTS, channels).transpose(2, 0, 1, 3, 4)
    blocks, coefs = lax.optimization_barrier((blocks, coefs))
    state = join(blocks, rows)
    states, kept = stage(0, 0, False, y_index, state, basis, coefs, None)
    basis = turn(basis)
    for step in range(1, planes):
        last = step == planes - 1
        for part in range(PARTS):
            state = lax.ppermute(states[part], "y", [(step - 1, step)])
            fresh, kept = stage(step, part, last, y_index, state, basis, coefs, kept)
            states[part] = None if last else fresh[0]
    back = lax.all_to_all(kept[:4].reshape(64, rows, lanes), PLANE, 0, 0)
    return finish(back.reshape(64, count, per, lanes))[None]


def solution(mesh):
    fine = Mesh(mesh.devices.reshape(SIZES), AXES)
    sec, ch = ("y", "x"), CH_AXES
    in_specs = (P(None, ch, None), P(), P(sec, ch), P(sec, ch, None))
    out_specs = P(sec, None, ch, None)
    return jax.shard_map(
        per_device, mesh=fine, in_specs=in_specs, out_specs=out_specs, check_vma=False
    )
```

```python
import functools

import jax
import jax.numpy as jnp
from jax import lax
from jax.experimental import pallas as pl
from jax.experimental.pallas import tpu as pltpu
from jax.sharding import Mesh
from jax.sharding import PartitionSpec as P

AXES = ("y", "x", "z", "core")
SIZES = (8, 4, 8, 2)
CH_AXES = ("z", "core")
PLANE = ("x", "z", "core")
MIB = 1024 * 1024
PARTS = 3


def spread_kernel(x_ref, v_ref, p_ref, limit_ref, out_ref):
    e = pl.program_id(0)
    both = jnp.concatenate([v_ref[0], p_ref[0]], axis=0).astype(jnp.float32)
    turned = both.T.astype(jnp.bfloat16)
    groups, _, per, lanes = out_ref.shape
    out_ref[...] = turned.reshape(groups, 1, per, lanes)

    @pl.when(e == pl.num_programs(0) - 1)
    def _():
        for k in range(groups):
            out_ref[k, 0] = limit_ref[...]


def spread(x_index, start, limits):
    energies, rows, width = start.shape
    cols = width // 8
    per = cols // 16
    return pl.pallas_call(
        spread_kernel,
        grid_spec=pltpu.PrefetchScalarGridSpec(
            num_scalar_prefetch=1,
            grid=(energies + 1,),
            in_specs=[
                pl.BlockSpec((1, rows, cols), lambda e, x: (jnp.minimum(e, energies - 1), 0, x[0])),
                pl.BlockSpec((1, rows, cols), lambda e, x: (jnp.minimum(e, energies - 1), 0, 4 + x[0])),
                pl.BlockSpec(limits.shape, lambda e, x: (0, 0)),
            ],
            out_specs=pl.BlockSpec((16, 1, per, 2 * rows), lambda e, x: (0, e, 0, 0)),
        ),
        out_shape=jax.ShapeDtypeStruct((16, energies + 1, per, 2 * rows), start.dtype),
        name="spread",
    )(x_index, start, start, limits)


def join_kernel(in_ref, out_ref):
    rows = out_ref.shape[1]
    low = lax.broadcasted_iota(jnp.int32, (rows, 128), 1) < 64
    for z in range(8):
        one = in_ref[2 * z, pl.ds(0, rows)].astype(jnp.float32)
        two = in_ref[2 * z + 1, pl.ds(0, rows)].astype(jnp.float32)
        lanes = pl.ds(128 * z, 128)
        out_ref[0, :, lanes] = jnp.where(low, one, pltpu.roll(two, 64, 1)).astype(out_ref.dtype)
        out_ref[1, :, lanes] = jnp.where(low, pltpu.roll(one, 64, 1), two).astype(out_ref.dtype)


def join(pieces, rows):
    return pl.pallas_call(
        join_kernel,
        out_shape=jax.ShapeDtypeStruct((2, rows, 1024), pieces.dtype),
        compiler_params=pltpu.CompilerParams(vmem_limit_bytes=8 * MIB),
        name="join",
    )(pieces)


def turn_kernel(*refs):
    out_ref = refs[-1]
    for q, ref in enumerate(refs[:-1]):
        groups, _, share, channels = ref.shape
        block = ref[...].reshape(groups * share, channels)
        out_ref[0, :, pl.ds(groups * share * q, groups * share)] = block.T


def turn(basis):
    groups, sectors, share, channels = basis.shape
    part = groups // 4
    specs = [pl.BlockSpec((part, 1, share, channels), lambda s, q=q: (q, s, 0, 0)) for q in range(4)]
    return pl.pallas_call(
        turn_kernel,
        grid=(sectors,),
        in_specs=specs,
        out_specs=pl.BlockSpec((1, channels, groups * share), lambda s: (s, 0, 0)),
        out_shape=jax.ShapeDtypeStruct((sectors, channels, groups * share), basis.dtype),
        compiler_params=pltpu.CompilerParams(vmem_limit_bytes=40 * MIB),
        cost_estimate=pl.CostEstimate(flops=0, bytes_accessed=2 * basis.size, transcendentals=0),
        name="turn",
    )(basis, basis, basis, basis)


def rotate(now, rot, coef_ref, part, sector, first_row, rows, per):
    for e in range(coef_ref.shape[3]):
        cosine = coef_ref[part, sector, 0, pl.ds(e, 1), :]
        ratio = coef_ref[part, sector, 1, pl.ds(e, 1), :]
        product = coef_ref[part, sector, 2, pl.ds(e, 1), :]
        upper = pl.ds(first_row + per * e, per)
        lower = pl.ds(rows + first_row + per * e, per)
        values = now[upper, :].astype(jnp.float32)
        slopes = now[lower, :].astype(jnp.float32)
        rot[upper, :] = (cosine * values + ratio * slopes).astype(rot.dtype)
        rot[lower, :] = (cosine * slopes - product * values).astype(rot.dtype)


def pair_up(fresh, rows, z):
    low = lax.broadcasted_iota(jnp.int32, (rows, 128), 1) < 64
    lanes = slice(128 * z, 128 * z + 128)
    values = fresh[:rows, lanes]
    slopes = fresh[rows:, lanes]
    one = jnp.where(low, values, pltpu.roll(slopes, 64, 1)).astype(jnp.bfloat16)
    two = jnp.where(low, pltpu.roll(values, 64, 1), slopes).astype(jnp.bfloat16)
    return one, two


def first_kernel(pieces, y_ref, state_ref, *refs):
    basis_refs, coef_ref = refs[:pieces], refs[pieces]
    next_refs, (kept_ref, now, rot) = refs[pieces + 1 : -3], refs[-3:]
    s = pl.program_id(0)
    rows, channels = state_ref.shape[1:]
    own = rows // PARTS
    per = own // coef_ref.shape[3]

    @pl.when(y_ref[0] == 0)
    def _():
        @pl.when(s == 0)
        def _():
            now[pl.ds(0, rows)] = state_ref[0]
            now[pl.ds(rows, rows)] = state_ref[1]

        for part in range(PARTS):
            rotate(now, rot, coef_ref, part, 0, own * part, rows, per)
        width = channels // pieces
        for q, basis_ref in enumerate(basis_refs):
            block = basis_ref[...].reshape(width, channels)
            fresh = lax.dot_general(
                rot[...], block, (((1,), (1,)), ((), ())), preferred_element_type=jnp.float32
            )
            now[:, pl.ds(width * q, width)] = fresh.astype(now.dtype)
            for k in range(width // 128):
                z = width // 128 * q + k
                one, two = pair_up(fresh, rows, k)
                kept_ref[0, 2 * z] = one.reshape(PARTS, own, 128)
                kept_ref[0, 2 * z + 1] = two.reshape(PARTS, own, 128)

        @pl.when(s == pl.num_programs(0) - 1)
        def _():
            for part, next_ref in enumerate(next_refs):
                next_ref[0] = now[pl.ds(own * part, own)]
                next_ref[1] = now[pl.ds(rows + own * part, own)]


def first_stage(y_index, state, basis, coefs):
    sectors = coefs.shape[1]
    _, rows, channels = state.shape
    pieces = 4
    own = rows // PARTS
    groups, _, share, _ = basis.shape
    block = (groups // pieces, 1, share, channels)
    outs = pl.pallas_call(
        functools.partial(first_kernel, pieces),
        grid_spec=pltpu.PrefetchScalarGridSpec(
            num_scalar_prefetch=1,
            grid=(sectors,),
            in_specs=[pl.BlockSpec(state.shape, lambda s, y: (0, 0, 0))]
            + [pl.BlockSpec(block, lambda s, y, q=q: (q, s, 0, 0)) for q in range(pieces)]
            + [pl.BlockSpec((PARTS, 1) + coefs.shape[2:], lambda s, y: (0, s, 0, 0, 0))],
            out_specs=[pl.BlockSpec((2, own, channels), lambda s, y: (0, 0, 0))] * PARTS
            + [pl.BlockSpec((1, groups, PARTS, own, 128), lambda s, y: (s, 0, 0, 0, 0))],
            scratch_shapes=[pltpu.VMEM((2 * rows, channels), state.dtype)] * 2,
        ),
        out_shape=[jax.ShapeDtypeStruct((2, own, channels), state.dtype)] * PARTS
        + [jax.ShapeDtypeStruct((sectors, groups, PARTS, own, 128), state.dtype)],
        compiler_params=pltpu.CompilerParams(vmem_limit_bytes=48 * MIB),
        cost_estimate=pl.CostEstimate(
            flops=4 * sectors * rows * channels * channels,
            bytes_accessed=2 * sectors * channels * (channels + 2 * rows),
            transcendentals=0,
        ),
        name="first_stage",
    )(y_index, state, *[basis] * pieces, coefs)
    return list(outs[:-1]), outs[-1]


def stage_kernel(step, part, y_ref, state_ref, basis_ref, coef_ref, *refs):
    next_refs, (kept_ref, now, rot) = refs[1:-3], refs[-3:]
    rows, channels = state_ref.shape[1:]
    sectors = basis_ref.shape[0]
    per = rows // coef_ref.shape[3]

    @pl.when(y_ref[0] == step)
    def _():
        now[pl.ds(0, rows)] = state_ref[0]
        now[pl.ds(rows, rows)] = state_ref[1]
        for s in range(sectors):
            rotate(now, rot, coef_ref, part, s, 0, rows, per)
            fresh = jnp.dot(rot[...], basis_ref[s], preferred_element_type=jnp.float32)
            if s < sectors - 1 or next_refs:
                now[...] = fresh.astype(now.dtype)
            for z in range(channels // 128):
                kept_ref[s, 2 * z, part], kept_ref[s, 2 * z + 1, part] = pair_up(fresh, rows, z)
        for next_ref in next_refs:
            next_ref[0] = now[pl.ds(0, rows)]
            next_ref[1] = now[pl.ds(rows, rows)]


def stage(step, part, last, y_index, state, basis, coefs, kept):
    sectors = coefs.shape[1]
    _, rows, channels = state.shape
    handed = 0 if last else 1
    whole = pl.BlockSpec(memory_space=pltpu.VMEM)
    return pl.pallas_call(
        functools.partial(stage_kernel, step, part),
        in_specs=[pl.BlockSpec(memory_space=pltpu.SMEM)] + [whole] * 4,
        out_specs=[whole] * (handed + 1),
        out_shape=[jax.ShapeDtypeStruct(state.shape, state.dtype)] * handed
        + [jax.ShapeDtypeStruct(kept.shape, kept.dtype)],
        scratch_shapes=[pltpu.VMEM((2 * rows, channels), state.dtype)] * 2,
        input_output_aliases={4: handed},
        compiler_params=pltpu.CompilerParams(vmem_limit_bytes=24 * MIB),
        cost_estimate=pl.CostEstimate(
            flops=4 * sectors * rows * channels * channels,
            bytes_accessed=2 * sectors * channels * (channels + 2 * rows),
            transcendentals=0,
        ),
        name="stage",
    )(y_index, state, basis, coefs, kept)


def finish_kernel(in_ref, out_ref):
    groups, energies, per, lanes = in_ref.shape
    half = lanes // 2
    cols = groups * per
    for e in range(energies):
        turned = in_ref[:, e].reshape(cols, lanes).T
        out_ref[e, :, pl.ds(0, cols)] = turned[:half]
        out_ref[e, :, pl.ds(cols, cols)] = turned[half:]


def finish(pieces):
    groups, energies, per, lanes = pieces.shape
    batch = 2
    return pl.pallas_call(
        finish_kernel,
        grid=(energies // batch,),
        in_specs=[pl.BlockSpec((groups, batch, per, lanes), lambda e: (0, e, 0, 0))],
        out_specs=pl.BlockSpec((batch, lanes // 2, 2 * groups * per), lambda e: (e, 0, 0)),
        out_shape=jax.ShapeDtypeStruct((energies, lanes // 2, 2 * groups * per), pieces.dtype),
        compiler_params=pltpu.CompilerParams(vmem_limit_bytes=16 * MIB),
        name="finish",
    )(pieces)


def per_device(start_amps, energies, thresholds, intersection):
    planes = lax.axis_size("y")
    y_index = lax.axis_index("y").astype(jnp.int32).reshape(1)
    x_index = lax.axis_index("x").astype(jnp.int32).reshape(1)
    count = energies.shape[0]
    channels = intersection.shape[2]
    share = intersection.shape[1]
    extra = jnp.pad(thresholds, ((0, 7), (0, channels - share)))
    ring = lax.all_gather(jnp.concatenate([intersection[0], extra]), "x")
    basis = lax.all_gather(ring[:, :share], CH_AXES)
    limits = jnp.pad(ring[:, share, :share].reshape(2, 2 * share), ((0, 14), (0, 0)))

    blocks = spread(x_index, start_amps, limits)
    per, lanes = blocks.shape[2:]
    rows = count * per
    blocks = lax.all_to_all(blocks.reshape(16, rows + per, lanes), CH_AXES, 0, 0)
    limits = blocks[:, rows : rows + 2].reshape(16, 4, share).swapaxes(0, 1).reshape(4, 1, channels)
    wave = jnp.sqrt(energies[None, :, None] - limits.astype(jnp.float32))
    sine = jnp.sin(wave)
    coefs = jnp.stack([jnp.cos(wave), sine / wave, wave * sine], axis=1)
    coefs = coefs.reshape(4, 3, PARTS, count // PARTS, channels).transpose(2, 0, 1, 3, 4)
    blocks, coefs = lax.optimization_barrier((blocks, coefs))
    state = join(blocks, rows)
    states, kept = first_stage(y_index, state, basis, coefs)
    basis = turn(basis)
    for step in range(1, planes):
        last = step == planes - 1
        for part in range(PARTS):
            state = lax.ppermute(states[part], "y", [(step - 1, step)])
            *fresh, kept = stage(step, part, last, y_index, state, basis, coefs, kept)
            states[part] = None if last else fresh[0]
    back = lax.all_to_all(kept.reshape(64, rows, lanes), PLANE, 0, 0)
    return finish(back.reshape(64, count, per, lanes))[None]


def solution(mesh):
    fine = Mesh(mesh.devices.reshape(SIZES), AXES)
    sec, ch = ("y", "x"), CH_AXES
    in_specs = (P(None, ch, None), P(), P(sec, ch), P(sec, ch, None))
    out_specs = P(sec, None, ch, None)
    return jax.shard_map(
        per_device, mesh=fine, in_specs=in_specs, out_specs=out_specs, check_vma=False
    )
```

```python
import functools

import jax
import jax.numpy as jnp
from jax import lax
from jax.experimental import pallas as pl
from jax.experimental.pallas import tpu as pltpu
from jax.sharding import Mesh
from jax.sharding import PartitionSpec as P

AXES = ("y", "x", "z", "core")
SIZES = (8, 4, 8, 2)
CH_AXES = ("z", "core")
PLANE = ("x", "z", "core")
MIB = 1024 * 1024
PARTS = 3


def spread_kernel(x_ref, v_ref, p_ref, limit_ref, out_ref):
    e = pl.program_id(0)
    both = jnp.concatenate([v_ref[0], p_ref[0]], axis=0).astype(jnp.float32)
    turned = both.T.astype(jnp.bfloat16)
    groups, _, per, lanes = out_ref.shape
    out_ref[...] = turned.reshape(groups, 1, per, lanes)

    @pl.when(e == pl.num_programs(0) - 1)
    def _():
        for k in range(groups):
            out_ref[k, 0] = limit_ref[...]


def spread(x_index, start, limits):
    energies, rows, width = start.shape
    cols = width // 8
    per = cols // 16
    return pl.pallas_call(
        spread_kernel,
        grid_spec=pltpu.PrefetchScalarGridSpec(
            num_scalar_prefetch=1,
            grid=(energies + 1,),
            in_specs=[
                pl.BlockSpec((1, rows, cols), lambda e, x: (jnp.minimum(e, energies - 1), 0, x[0])),
                pl.BlockSpec((1, rows, cols), lambda e, x: (jnp.minimum(e, energies - 1), 0, 4 + x[0])),
                pl.BlockSpec(limits.shape, lambda e, x: (0, 0)),
            ],
            out_specs=pl.BlockSpec((16, 1, per, 2 * rows), lambda e, x: (0, e, 0, 0)),
        ),
        out_shape=jax.ShapeDtypeStruct((16, energies + 1, per, 2 * rows), start.dtype),
        name="spread",
    )(x_index, start, start, limits)


def join_kernel(in_ref, out_ref):
    rows = out_ref.shape[1]
    low = lax.broadcasted_iota(jnp.int32, (rows, 128), 1) < 64
    for z in range(8):
        one = in_ref[2 * z, pl.ds(0, rows)].astype(jnp.float32)
        two = in_ref[2 * z + 1, pl.ds(0, rows)].astype(jnp.float32)
        lanes = pl.ds(128 * z, 128)
        out_ref[0, :, lanes] = jnp.where(low, one, pltpu.roll(two, 64, 1)).astype(out_ref.dtype)
        out_ref[1, :, lanes] = jnp.where(low, pltpu.roll(one, 64, 1), two).astype(out_ref.dtype)


def join(pieces, rows):
    return pl.pallas_call(
        join_kernel,
        out_shape=jax.ShapeDtypeStruct((2, rows, 1024), pieces.dtype),
        compiler_params=pltpu.CompilerParams(vmem_limit_bytes=8 * MIB),
        name="join",
    )(pieces)


def turn_kernel(*refs):
    out_ref = refs[-1]
    for q, ref in enumerate(refs[:-1]):
        groups, _, share, channels = ref.shape
        block = ref[...].reshape(groups * share, channels)
        out_ref[0, :, pl.ds(groups * share * q, groups * share)] = block.T


def turn(basis):
    groups, sectors, share, channels = basis.shape
    part = groups // 4
    specs = [pl.BlockSpec((part, 1, share, channels), lambda s, q=q: (q, s, 0, 0)) for q in range(4)]
    return pl.pallas_call(
        turn_kernel,
        grid=(sectors,),
        in_specs=specs,
        out_specs=pl.BlockSpec((1, channels, groups * share), lambda s: (s, 0, 0)),
        out_shape=jax.ShapeDtypeStruct((sectors, channels, groups * share), basis.dtype),
        compiler_params=pltpu.CompilerParams(vmem_limit_bytes=40 * MIB),
        cost_estimate=pl.CostEstimate(flops=0, bytes_accessed=2 * basis.size, transcendentals=0),
        name="turn",
    )(basis, basis, basis, basis)


def rotate(now, rot, coef_ref, part, sector, first_row, rows, per):
    for e in range(coef_ref.shape[3]):
        cosine = coef_ref[part, sector, 0, pl.ds(e, 1), :]
        ratio = coef_ref[part, sector, 1, pl.ds(e, 1), :]
        product = coef_ref[part, sector, 2, pl.ds(e, 1), :]
        upper = pl.ds(first_row + per * e, per)
        lower = pl.ds(rows + first_row + per * e, per)
        values = now[upper, :].astype(jnp.float32)
        slopes = now[lower, :].astype(jnp.float32)
        rot[upper, :] = (cosine * values + ratio * slopes).astype(rot.dtype)
        rot[lower, :] = (cosine * slopes - product * values).astype(rot.dtype)


def pair_up(fresh, rows, z):
    low = lax.broadcasted_iota(jnp.int32, (rows, 128), 1) < 64
    lanes = slice(128 * z, 128 * z + 128)
    values = fresh[:rows, lanes]
    slopes = fresh[rows:, lanes]
    one = jnp.where(low, values, pltpu.roll(slopes, 64, 1)).astype(jnp.bfloat16)
    two = jnp.where(low, pltpu.roll(values, 64, 1), slopes).astype(jnp.bfloat16)
    return one, two


def first_kernel(pieces, y_ref, state_ref, *refs):
    basis_refs, coef_ref = refs[:pieces], refs[pieces]
    next_refs, (kept_ref, now, rot) = refs[pieces + 1 : -3], refs[-3:]
    s = pl.program_id(0)
    rows, channels = state_ref.shape[1:]
    own = rows // PARTS
    per = own // coef_ref.shape[3]

    @pl.when(y_ref[0] == 0)
    def _():
        @pl.when(s == 0)
        def _():
            now[pl.ds(0, rows)] = state_ref[0]
            now[pl.ds(rows, rows)] = state_ref[1]

        for part in range(PARTS):
            rotate(now, rot, coef_ref, part, 0, own * part, rows, per)
        width = channels // pieces
        for q, basis_ref in enumerate(basis_refs):
            block = basis_ref[...].reshape(width, channels)
            fresh = lax.dot_general(
                rot[...], block, (((1,), (1,)), ((), ())), preferred_element_type=jnp.float32
            )
            now[:, pl.ds(width * q, width)] = fresh.astype(now.dtype)
            for k in range(width // 128):
                z = width // 128 * q + k
                one, two = pair_up(fresh, rows, k)
                kept_ref[0, 2 * z] = one.reshape(PARTS, own, 128)
                kept_ref[0, 2 * z + 1] = two.reshape(PARTS, own, 128)

        @pl.when(s == pl.num_programs(0) - 1)
        def _():
            for part, next_ref in enumerate(next_refs):
                next_ref[0] = now[pl.ds(own * part, own)]
                next_ref[1] = now[pl.ds(rows + own * part, own)]


def first_stage(y_index, state, basis, coefs):
    sectors = coefs.shape[1]
    _, rows, channels = state.shape
    pieces = 4
    own = rows // PARTS
    groups, _, share, _ = basis.shape
    block = (groups // pieces, 1, share, channels)
    outs = pl.pallas_call(
        functools.partial(first_kernel, pieces),
        grid_spec=pltpu.PrefetchScalarGridSpec(
            num_scalar_prefetch=1,
            grid=(sectors,),
            in_specs=[pl.BlockSpec(state.shape, lambda s, y: (0, 0, 0))]
            + [pl.BlockSpec(block, lambda s, y, q=q: (q, s, 0, 0)) for q in range(pieces)]
            + [pl.BlockSpec((PARTS, 1) + coefs.shape[2:], lambda s, y: (0, s, 0, 0, 0))],
            out_specs=[pl.BlockSpec((2, own, channels), lambda s, y: (0, 0, 0))] * PARTS
            + [pl.BlockSpec((1, groups, PARTS, own, 128), lambda s, y: (s, 0, 0, 0, 0))],
            scratch_shapes=[pltpu.VMEM((2 * rows, channels), state.dtype)] * 2,
        ),
        out_shape=[jax.ShapeDtypeStruct((2, own, channels), state.dtype)] * PARTS
        + [jax.ShapeDtypeStruct((sectors, groups, PARTS, own, 128), state.dtype)],
        compiler_params=pltpu.CompilerParams(vmem_limit_bytes=48 * MIB),
        cost_estimate=pl.CostEstimate(
            flops=4 * sectors * rows * channels * channels,
            bytes_accessed=2 * sectors * channels * (channels + 2 * rows),
            transcendentals=0,
        ),
        name="first_stage",
    )(y_index, state, *[basis] * pieces, coefs)
    return list(outs[:-1]), outs[-1]


def stage_kernel(step, part, y_ref, state_ref, basis_ref, coef_ref, *refs):
    next_refs, (kept_ref, now, rot) = refs[1:-3], refs[-3:]
    rows, channels = state_ref.shape[1:]
    sectors = basis_ref.shape[0]
    per = rows // coef_ref.shape[3]

    @pl.when(y_ref[0] == step)
    def _():
        now[pl.ds(0, rows)] = state_ref[0]
        now[pl.ds(rows, rows)] = state_ref[1]
        for s in range(sectors):
            rotate(now, rot, coef_ref, part, s, 0, rows, per)
            fresh = jnp.dot(rot[...], basis_ref[s], preferred_element_type=jnp.float32)
            if s < sectors - 1 or next_refs:
                now[...] = fresh.astype(now.dtype)
            for z in range(channels // 128):
                kept_ref[s, 2 * z, part], kept_ref[s, 2 * z + 1, part] = pair_up(fresh, rows, z)
        for next_ref in next_refs:
            next_ref[0] = now[pl.ds(0, rows)]
            next_ref[1] = now[pl.ds(rows, rows)]


def stage(step, part, last, y_index, state, basis, coefs, kept):
    sectors = coefs.shape[1]
    _, rows, channels = state.shape
    handed = 0 if last else 1
    whole = pl.BlockSpec(memory_space=pltpu.VMEM)
    return pl.pallas_call(
        functools.partial(stage_kernel, step, part),
        in_specs=[pl.BlockSpec(memory_space=pltpu.SMEM)] + [whole] * 4,
        out_specs=[whole] * (handed + 1),
        out_shape=[jax.ShapeDtypeStruct(state.shape, state.dtype)] * handed
        + [jax.ShapeDtypeStruct(kept.shape, kept.dtype)],
        scratch_shapes=[pltpu.VMEM((2 * rows, channels), state.dtype)] * 2,
        input_output_aliases={4: handed},
        compiler_params=pltpu.CompilerParams(vmem_limit_bytes=24 * MIB),
        cost_estimate=pl.CostEstimate(
            flops=4 * sectors * rows * channels * channels,
            bytes_accessed=2 * sectors * channels * (channels + 2 * rows),
            transcendentals=0,
        ),
        name="stage",
    )(y_index, state, basis, coefs, kept)


def finish_kernel(in_ref, out_ref):
    groups, _, per, lanes = in_ref.shape
    half = lanes // 2
    cols = groups * per
    turned = in_ref[:, pl.program_id(0)].reshape(cols, lanes).T
    out_ref[0, :, pl.ds(0, cols)] = turned[:half]
    out_ref[0, :, pl.ds(cols, cols)] = turned[half:]


def finish(pieces):
    groups, energies, per, lanes = pieces.shape
    return pl.pallas_call(
        finish_kernel,
        grid=(energies,),
        in_specs=[pl.BlockSpec(memory_space=pltpu.VMEM)],
        out_specs=pl.BlockSpec((1, lanes // 2, 2 * groups * per), lambda e: (e, 0, 0)),
        out_shape=jax.ShapeDtypeStruct((energies, lanes // 2, 2 * groups * per), pieces.dtype),
        compiler_params=pltpu.CompilerParams(vmem_limit_bytes=16 * MIB),
        name="finish",
    )(pieces)


def per_device(start_amps, energies, thresholds, intersection):
    planes = lax.axis_size("y")
    y_index = lax.axis_index("y").astype(jnp.int32).reshape(1)
    x_index = lax.axis_index("x").astype(jnp.int32).reshape(1)
    count = energies.shape[0]
    channels = intersection.shape[2]
    share = intersection.shape[1]
    extra = jnp.pad(thresholds, ((0, 7), (0, channels - share)))
    ring = lax.all_gather(jnp.concatenate([intersection[0], extra]), "x")
    basis = lax.all_gather(ring[:, :share], CH_AXES)
    limits = jnp.pad(ring[:, share, :share].reshape(2, 2 * share), ((0, 14), (0, 0)))

    blocks = spread(x_index, start_amps, limits)
    per, lanes = blocks.shape[2:]
    rows = count * per
    blocks = lax.all_to_all(blocks.reshape(16, rows + per, lanes), CH_AXES, 0, 0)
    limits = blocks[:, rows : rows + 2].reshape(16, 4, share).swapaxes(0, 1).reshape(4, 1, channels)
    wave = jnp.sqrt(energies[None, :, None] - limits.astype(jnp.float32))
    sine = jnp.sin(wave)
    coefs = jnp.stack([jnp.cos(wave), sine / wave, wave * sine], axis=1)
    coefs = coefs.reshape(4, 3, PARTS, count // PARTS, channels).transpose(2, 0, 1, 3, 4)
    blocks, coefs = lax.optimization_barrier((blocks, coefs))
    state = join(blocks, rows)
    states, kept = first_stage(y_index, state, basis, coefs)
    basis = turn(basis)
    for step in range(1, planes):
        last = step == planes - 1
        for part in range(PARTS):
            state = lax.ppermute(states[part], "y", [(step - 1, step)])
            *fresh, kept = stage(step, part, last, y_index, state, basis, coefs, kept)
            states[part] = None if last else fresh[0]
    back = lax.all_to_all(kept.reshape(64, rows, lanes), PLANE, 0, 0)
    return finish(back.reshape(64, count, per, lanes))[None]


def solution(mesh):
    fine = Mesh(mesh.devices.reshape(SIZES), AXES)
    sec, ch = ("y", "x"), CH_AXES
    in_specs = (P(None, ch, None), P(), P(sec, ch), P(sec, ch, None))
    out_specs = P(sec, None, ch, None)
    return jax.shard_map(
        per_device, mesh=fine, in_specs=in_specs, out_specs=out_specs, check_vma=False
    )
```

```python
import functools

import jax
import jax.numpy as jnp
from jax import lax
from jax.experimental import pallas as pl
from jax.experimental.pallas import tpu as pltpu
from jax.sharding import Mesh
from jax.sharding import PartitionSpec as P

AXES = ("y", "x", "z", "core")
SIZES = (8, 4, 8, 2)
CH_AXES = ("z", "core")
PLANE = ("x", "z", "core")
MIB = 1024 * 1024
PARTS = 3


def spread_kernel(x_ref, v_ref, p_ref, limit_ref, out_ref):
    e = pl.program_id(0)
    both = jnp.concatenate([v_ref[0], p_ref[0]], axis=0).astype(jnp.float32)
    turned = both.T.astype(jnp.bfloat16)
    groups, _, per, lanes = out_ref.shape
    out_ref[...] = turned.reshape(groups, 1, per, lanes)

    @pl.when(e == pl.num_programs(0) - 1)
    def _():
        for k in range(groups):
            out_ref[k, 0] = limit_ref[...]


def spread(x_index, start, limits):
    energies, rows, width = start.shape
    cols = width // 8
    per = cols // 16
    return pl.pallas_call(
        spread_kernel,
        grid_spec=pltpu.PrefetchScalarGridSpec(
            num_scalar_prefetch=1,
            grid=(energies + 1,),
            in_specs=[
                pl.BlockSpec((1, rows, cols), lambda e, x: (jnp.minimum(e, energies - 1), 0, x[0])),
                pl.BlockSpec((1, rows, cols), lambda e, x: (jnp.minimum(e, energies - 1), 0, 4 + x[0])),
                pl.BlockSpec(limits.shape, lambda e, x: (0, 0)),
            ],
            out_specs=pl.BlockSpec((16, 1, per, 2 * rows), lambda e, x: (0, e, 0, 0)),
        ),
        out_shape=jax.ShapeDtypeStruct((16, energies + 1, per, 2 * rows), start.dtype),
        name="spread",
    )(x_index, start, start, limits)


def join_kernel(in_ref, out_ref):
    rows = out_ref.shape[1]
    low = lax.broadcasted_iota(jnp.int32, (rows, 128), 1) < 64
    for z in range(8):
        one = in_ref[2 * z, pl.ds(0, rows)].astype(jnp.float32)
        two = in_ref[2 * z + 1, pl.ds(0, rows)].astype(jnp.float32)
        lanes = pl.ds(128 * z, 128)
        out_ref[0, :, lanes] = jnp.where(low, one, pltpu.roll(two, 64, 1)).astype(out_ref.dtype)
        out_ref[1, :, lanes] = jnp.where(low, pltpu.roll(one, 64, 1), two).astype(out_ref.dtype)


def join(pieces, rows):
    return pl.pallas_call(
        join_kernel,
        out_shape=jax.ShapeDtypeStruct((2, rows, 1024), pieces.dtype),
        compiler_params=pltpu.CompilerParams(vmem_limit_bytes=8 * MIB),
        name="join",
    )(pieces)


def turn_kernel(*refs):
    out_ref = refs[-1]
    for q, ref in enumerate(refs[:-1]):
        groups, _, share, channels = ref.shape
        block = ref[...].reshape(groups * share, channels)
        out_ref[0, :, pl.ds(groups * share * q, groups * share)] = block.T


def turn(basis):
    groups, sectors, share, channels = basis.shape
    part = groups // 4
    specs = [pl.BlockSpec((part, 1, share, channels), lambda s, q=q: (q, s, 0, 0)) for q in range(4)]
    return pl.pallas_call(
        turn_kernel,
        grid=(sectors,),
        in_specs=specs,
        out_specs=pl.BlockSpec((1, channels, groups * share), lambda s: (s, 0, 0)),
        out_shape=jax.ShapeDtypeStruct((sectors, channels, groups * share), basis.dtype),
        compiler_params=pltpu.CompilerParams(vmem_limit_bytes=40 * MIB),
        cost_estimate=pl.CostEstimate(flops=0, bytes_accessed=2 * basis.size, transcendentals=0),
        name="turn",
    )(basis, basis, basis, basis)


def rotate(now, rot, coef_ref, part, sector, first_row, rows, per):
    for e in range(coef_ref.shape[3]):
        cosine = coef_ref[part, sector, 0, pl.ds(e, 1), :]
        ratio = coef_ref[part, sector, 1, pl.ds(e, 1), :]
        product = coef_ref[part, sector, 2, pl.ds(e, 1), :]
        upper = pl.ds(first_row + per * e, per)
        lower = pl.ds(rows + first_row + per * e, per)
        values = now[upper, :].astype(jnp.float32)
        slopes = now[lower, :].astype(jnp.float32)
        rot[upper, :] = (cosine * values + ratio * slopes).astype(rot.dtype)
        rot[lower, :] = (cosine * slopes - product * values).astype(rot.dtype)


def pair_up(fresh, rows, z):
    low = lax.broadcasted_iota(jnp.int32, (rows, 128), 1) < 64
    lanes = slice(128 * z, 128 * z + 128)
    values = fresh[:rows, lanes]
    slopes = fresh[rows:, lanes]
    one = jnp.where(low, values, pltpu.roll(slopes, 64, 1)).astype(jnp.bfloat16)
    two = jnp.where(low, pltpu.roll(values, 64, 1), slopes).astype(jnp.bfloat16)
    return one, two


def first_kernel(pieces, y_ref, state_ref, *refs):
    basis_refs, coef_ref = refs[:pieces], refs[pieces]
    next_refs, (kept_ref, now, rot) = refs[pieces + 1 : -3], refs[-3:]
    s = pl.program_id(0)
    rows, channels = state_ref.shape[1:]
    own = rows // PARTS
    per = own // coef_ref.shape[3]

    @pl.when(y_ref[0] == 0)
    def _():
        @pl.when(s == 0)
        def _():
            now[pl.ds(0, rows)] = state_ref[0]
            now[pl.ds(rows, rows)] = state_ref[1]

        for part in range(PARTS):
            rotate(now, rot, coef_ref, part, 0, own * part, rows, per)
        width = channels // pieces
        blocks = [ref[...].reshape(width, channels) for ref in basis_refs]
        fresh = lax.dot_general(
            rot[...],
            jnp.concatenate(blocks, axis=0),
            (((1,), (1,)), ((), ())),
            preferred_element_type=jnp.float32,
        )
        now[...] = fresh.astype(now.dtype)
        for z in range(channels // 128):
            one, two = pair_up(fresh, rows, z)
            kept_ref[0, 2 * z] = one.reshape(PARTS, own, 128)
            kept_ref[0, 2 * z + 1] = two.reshape(PARTS, own, 128)

        @pl.when(s == pl.num_programs(0) - 1)
        def _():
            for part, next_ref in enumerate(next_refs):
                next_ref[0] = now[pl.ds(own * part, own)]
                next_ref[1] = now[pl.ds(rows + own * part, own)]


def first_stage(y_index, state, basis, coefs):
    sectors = coefs.shape[1]
    _, rows, channels = state.shape
    pieces = 4
    own = rows // PARTS
    groups, _, share, _ = basis.shape
    block = (groups // pieces, 1, share, channels)
    outs = pl.pallas_call(
        functools.partial(first_kernel, pieces),
        grid_spec=pltpu.PrefetchScalarGridSpec(
            num_scalar_prefetch=1,
            grid=(sectors,),
            in_specs=[pl.BlockSpec(state.shape, lambda s, y: (0, 0, 0))]
            + [pl.BlockSpec(block, lambda s, y, q=q: (q, s, 0, 0)) for q in range(pieces)]
            + [pl.BlockSpec((PARTS, 1) + coefs.shape[2:], lambda s, y: (0, s, 0, 0, 0))],
            out_specs=[pl.BlockSpec((2, own, channels), lambda s, y: (0, 0, 0))] * PARTS
            + [pl.BlockSpec((1, groups, PARTS, own, 128), lambda s, y: (s, 0, 0, 0, 0))],
            scratch_shapes=[pltpu.VMEM((2 * rows, channels), state.dtype)] * 2,
        ),
        out_shape=[jax.ShapeDtypeStruct((2, own, channels), state.dtype)] * PARTS
        + [jax.ShapeDtypeStruct((sectors, groups, PARTS, own, 128), state.dtype)],
        compiler_params=pltpu.CompilerParams(vmem_limit_bytes=48 * MIB),
        cost_estimate=pl.CostEstimate(
            flops=4 * sectors * rows * channels * channels,
            bytes_accessed=2 * sectors * channels * (channels + 2 * rows),
            transcendentals=0,
        ),
        name="first_stage",
    )(y_index, state, *[basis] * pieces, coefs)
    return list(outs[:-1]), outs[-1]


def stage_kernel(step, part, y_ref, state_ref, basis_ref, coef_ref, *refs):
    next_refs, (kept_ref, now, rot) = refs[1:-3], refs[-3:]
    rows, channels = state_ref.shape[1:]
    sectors = basis_ref.shape[0]
    per = rows // coef_ref.shape[3]

    @pl.when(y_ref[0] == step)
    def _():
        now[pl.ds(0, rows)] = state_ref[0]
        now[pl.ds(rows, rows)] = state_ref[1]
        for s in range(sectors):
            rotate(now, rot, coef_ref, part, s, 0, rows, per)
            fresh = jnp.dot(rot[...], basis_ref[s], preferred_element_type=jnp.float32)
            if s < sectors - 1 or next_refs:
                now[...] = fresh.astype(now.dtype)
            for z in range(channels // 128):
                kept_ref[s, 2 * z, part], kept_ref[s, 2 * z + 1, part] = pair_up(fresh, rows, z)
        for next_ref in next_refs:
            next_ref[0] = now[pl.ds(0, rows)]
            next_ref[1] = now[pl.ds(rows, rows)]


def stage(step, part, last, y_index, state, basis, coefs, kept):
    sectors = coefs.shape[1]
    _, rows, channels = state.shape
    handed = 0 if last else 1
    whole = pl.BlockSpec(memory_space=pltpu.VMEM)
    return pl.pallas_call(
        functools.partial(stage_kernel, step, part),
        in_specs=[pl.BlockSpec(memory_space=pltpu.SMEM)] + [whole] * 4,
        out_specs=[whole] * (handed + 1),
        out_shape=[jax.ShapeDtypeStruct(state.shape, state.dtype)] * handed
        + [jax.ShapeDtypeStruct(kept.shape, kept.dtype)],
        scratch_shapes=[pltpu.VMEM((2 * rows, channels), state.dtype)] * 2,
        input_output_aliases={4: handed},
        compiler_params=pltpu.CompilerParams(vmem_limit_bytes=24 * MIB),
        cost_estimate=pl.CostEstimate(
            flops=4 * sectors * rows * channels * channels,
            bytes_accessed=2 * sectors * channels * (channels + 2 * rows),
            transcendentals=0,
        ),
        name="stage",
    )(y_index, state, basis, coefs, kept)


def finish_kernel(in_ref, out_ref):
    groups, _, per, lanes = in_ref.shape
    batch = out_ref.shape[0]
    half = lanes // 2
    cols = groups * per
    for e in range(batch):
        block = in_ref[:, batch * pl.program_id(0) + e]
        turned = block.reshape(cols, lanes).T
        out_ref[e, :, pl.ds(0, cols)] = turned[:half]
        out_ref[e, :, pl.ds(cols, cols)] = turned[half:]


def finish(pieces):
    groups, energies, per, lanes = pieces.shape
    batch = 2
    return pl.pallas_call(
        finish_kernel,
        grid=(energies // batch,),
        in_specs=[pl.BlockSpec(memory_space=pltpu.VMEM)],
        out_specs=pl.BlockSpec((batch, lanes // 2, 2 * groups * per), lambda e: (e, 0, 0)),
        out_shape=jax.ShapeDtypeStruct((energies, lanes // 2, 2 * groups * per), pieces.dtype),
        compiler_params=pltpu.CompilerParams(vmem_limit_bytes=16 * MIB),
        name="finish",
    )(pieces)


def per_device(start_amps, energies, thresholds, intersection):
    planes = lax.axis_size("y")
    y_index = lax.axis_index("y").astype(jnp.int32).reshape(1)
    x_index = lax.axis_index("x").astype(jnp.int32).reshape(1)
    count = energies.shape[0]
    channels = intersection.shape[2]
    share = intersection.shape[1]
    extra = jnp.pad(thresholds, ((0, 7), (0, channels - share)))
    ring = lax.all_gather(jnp.concatenate([intersection[0], extra]), "x")
    basis = lax.all_gather(ring[:, :share], CH_AXES)
    limits = jnp.pad(ring[:, share, :share].reshape(2, 2 * share), ((0, 14), (0, 0)))

    blocks = spread(x_index, start_amps, limits)
    per, lanes = blocks.shape[2:]
    rows = count * per
    blocks = lax.all_to_all(blocks.reshape(16, rows + per, lanes), CH_AXES, 0, 0)
    limits = blocks[:, rows : rows + 2].reshape(16, 4, share).swapaxes(0, 1).reshape(4, 1, channels)
    wave = jnp.sqrt(energies[None, :, None] - limits.astype(jnp.float32))
    sine = jnp.sin(wave)
    coefs = jnp.stack([jnp.cos(wave), sine / wave, wave * sine], axis=1)
    coefs = coefs.reshape(4, 3, PARTS, count // PARTS, channels).transpose(2, 0, 1, 3, 4)
    blocks, coefs = lax.optimization_barrier((blocks, coefs))
    state = join(blocks, rows)
    states, kept = first_stage(y_index, state, basis, coefs)
    basis = turn(basis)
    for step in range(1, planes):
        last = step == planes - 1
        for part in range(PARTS):
            state = lax.ppermute(states[part], "y", [(step - 1, step)])
            *fresh, kept = stage(step, part, last, y_index, state, basis, coefs, kept)
            states[part] = None if last else fresh[0]
    back = lax.all_to_all(kept.reshape(64, rows, lanes), PLANE, 0, 0)
    return finish(back.reshape(64, count, per, lanes))[None]


def solution(mesh):
    fine = Mesh(mesh.devices.reshape(SIZES), AXES)
    sec, ch = ("y", "x"), CH_AXES
    in_specs = (P(None, ch, None), P(), P(sec, ch), P(sec, ch, None))
    out_specs = P(sec, None, ch, None)
    return jax.shard_map(
        per_device, mesh=fine, in_specs=in_specs, out_specs=out_specs, check_vma=False
    )
```
